128 devices in a mesh: lat: 8 (over z, core), ord: 16 (over x, y).
Axes of the slice: x: 4, y: 4, z: 4, core: 2. Of those that a mesh axis runs over, the one named last changes fastest.
Arguments:
- grid_field: float32 [1440, 768], P('ord', 'lat'), may hold values from -6 to 6
- legendre: bfloat16 [768, 720, 720], P('lat', 'ord'), may hold values from -0.21875 to 0.21875
- cycle_weight: float32 [768], P('lat'), may hold values from 0.2 to 2.4
- slot_order: int32 [720], replicated, may hold values from 0 to 719, each once
- kappa: float32 [8, 720], replicated, may hold values from 0.1 to 1
- eta: float32 [4, 2, 720], replicated, may hold values from -1 to 1
- pairs: int32 [2, 2], replicated, may hold values from 0 to 7
- target: float32 [2, 4], replicated, may hold values from -1 to 1
Outputs:
- gradient: float32 [1440, 768], P('ord', 'lat')
The draws below stay inside these ranges and needn't reach their ends.
Inputs may be any that keep to these rules, and one draw needn't show every extreme that they name: `slot_order`: a permutation of the orders.
All inputs are finite; a program needn't handle non-finite values.
Results may differ from the reference program's by a relative error of at most 0.0003.
Values sent between devices are 32-bit elements; how exact they have to be, the bound alone decides.
No kernel may reach another device: no remote copies, remote signals or barrier semaphores. Data moves between devices by JAX's collectives and lax.ppermute only.
A program may use at most 128 MiB of HBM per device.

```python
import math
import jax
import jax.numpy as jnp
from jax import lax

L = 720
NPHI = 1440
NTHETA = 768
SCALES = 8
DIRS = 4
PAIRS = 2


def draw_cycle_weight(key, part):
    key = jax.random.fold_in(key, 11)
    position = jnp.arange(NTHETA, dtype=jnp.float32) / NTHETA
    rough = jax.random.uniform(key, (NTHETA,), jnp.float32, 0.6, 1.4)
    base = 0.4 + 1.2 * position
    return (base * rough).astype(jnp.float32)


def place_ends(drawn, rng, smallest, largest):
    longest = drawn.shape.index(max(drawn.shape))
    spots = []
    for shift in (0, 1):
        where = [jax.random.randint(jax.random.fold_in(rng, axis), (), 0, length) for axis, length in enumerate(drawn.shape)]
        where[longest] = (where[longest] + shift) % drawn.shape[longest]
        spots.append(tuple(where))
    return drawn.at[spots[0]].set(smallest).at[spots[1]].set(largest)


def level_of(rng, extent, shards, low, top_value):
    gain, own = 1.0, jax.random.fold_in(rng, 6)
    for dim, parts in shards:
        heights = jnp.exp(jax.random.uniform(jax.random.fold_in(own, dim), (parts,), jnp.float32, low / len(shards), top_value / len(shards)))
        gain = gain * jnp.repeat(heights, extent[dim] // parts).reshape([-1 if axis == dim else 1 for axis in range(len(extent))])
    return gain


def bell_draw(key, dims, deviation, bound, cuts=(), held_as=jnp.bfloat16):
    array = jax.random.normal(key, dims, jnp.float32) * deviation
    if len(cuts) > 0:
        array = level_of(key, dims, cuts, -0.22, 0.18) * array
    return jnp.clip(array, min=-bound, max=bound).astype(held_as)


def setup_inputs(seed: int = 0) -> dict:
    arg_keys = jax.random.split(jax.random.key(seed), 9)
    grid_field = bell_draw(arg_keys[0], (NPHI, NTHETA), 1.0, 6.0, ((0, 16), (1, 8)), jnp.float32)
    legendre = bell_draw(arg_keys[1], (NTHETA, L, L), NTHETA ** -0.5, 0.21875, ((0, 8), (1, 16)))
    cycle_weight = draw_cycle_weight(jax.random.fold_in(arg_keys[8], 71), 0)
    slot_order = jax.random.permutation(arg_keys[3], L).astype(jnp.int32)
    kappa = jnp.clip(jnp.exp(jax.random.uniform(arg_keys[4], (SCALES, L), jnp.float32, math.log(0.1), math.log(1.0))), 0.1, 1.0)
    eta = jnp.clip(jax.random.uniform(arg_keys[5], (DIRS, 2, L), jnp.float32, -1.0, 1.0), -1.0, 1.0)
    pairs = place_ends(jax.random.randint(arg_keys[6], (PAIRS, 2), 0, SCALES), jax.random.fold_in(arg_keys[6], 1), 0, SCALES - 1).astype(jnp.int32)
    target = jnp.clip(jax.random.uniform(arg_keys[7], (PAIRS, DIRS), jnp.float32, -1.0, 1.0), -1.0, 1.0)
    return {"grid_field": grid_field, "legendre": legendre, "cycle_weight": cycle_weight, "slot_order": slot_order, "kappa": kappa, "eta": eta, "pairs": pairs, "target": target}


HIGHEST_PREC = lax.Precision.HIGHEST
MOD_EPSILON = 0.01

def make_waves(slot_order):
    longitude = jnp.arange(NPHI, dtype=jnp.int32)
    phase = slot_order[:, None] * longitude[None, :] % NPHI
    angles = phase.astype(jnp.float32) * (2.0 * math.pi / NPHI)
    return jnp.stack([jnp.cos(angles), jnp.sin(angles)])

def reference(grid_field, legendre, cycle_weight, slot_order, kappa, eta, pairs, target):
    harmonics = make_waves(slot_order)
    norming = math.sqrt(2.0 / NPHI)
    block_size = L // 8
    degree_ids = jnp.arange(L, dtype=jnp.int32)

    def table_block(index):
        part_table = lax.dynamic_slice_in_dim(legendre, index * block_size, block_size, 1).astype(jnp.float32)
        orders = lax.dynamic_slice_in_dim(slot_order, index * block_size, block_size, 0)
        keep = (degree_ids[None, :] >= orders[:, None]).astype(jnp.float32)
        return part_table * keep[None, :, :]

    def to_harm(fields, weighted):
        spectra = norming * jnp.einsum('qsk,bkt->bqst', harmonics, fields, precision=HIGHEST_PREC)
        if weighted:
            spectra = spectra * cycle_weight[None, None, None, :]

        def one_block(index):
            part_table = table_block(index)
            segment = lax.dynamic_slice_in_dim(spectra, index * block_size, block_size, 2)
            return jnp.einsum('tsl,bqst->bqls', part_table, segment, precision=HIGHEST_PREC)
        blocks = lax.map(one_block, jnp.arange(8, dtype=jnp.int32))
        return jnp.concatenate([blocks[index] for index in range(8)], axis=3)

    def to_grid(coeffs, weighted):

        def one_block(index):
            part_table = table_block(index)
            segment = lax.dynamic_slice_in_dim(coeffs, index * block_size, block_size, 3)
            return jnp.einsum('tsl,bqls->bqst', part_table, segment, precision=HIGHEST_PREC)
        blocks = lax.map(one_block, jnp.arange(8, dtype=jnp.int32))
        cycles = jnp.concatenate([blocks[index] for index in range(8)], axis=2)
        if weighted:
            cycles = cycles * cycle_weight[None, None, None, :]
        return norming * jnp.einsum('qsk,bqst->bkt', harmonics, cycles, precision=HIGHEST_PREC)
    eta_slots = eta[:, :, slot_order]
    kap_first = kappa[pairs[:, 0]]
    kap_second = kappa[pairs[:, 1]]

    def objective(field_in):
        base = to_harm(field_in[None], True)[0]
        first_coef = jnp.einsum('pl,drs,qls->pdrqls', kap_first, eta_slots, base, precision=HIGHEST_PREC)
        first_maps = to_grid(first_coef.reshape(PAIRS * DIRS * 2, 2, L, L), False).reshape(PAIRS, DIRS, 2, NPHI, NTHETA)
        pair_coef = jnp.einsum('pl,drs,qls->pdrqls', kap_second, eta_slots, base, precision=HIGHEST_PREC)
        pair_maps = to_grid(pair_coef.reshape(PAIRS * DIRS * 2, 2, L, L), False).reshape(PAIRS, DIRS, 2, NPHI, NTHETA)
        first_mod = jnp.sqrt(first_maps[:, :, 0] ** 2 + first_maps[:, :, 1] ** 2 + MOD_EPSILON)
        pair_mod = jnp.sqrt(pair_maps[:, :, 0] ** 2 + pair_maps[:, :, 1] ** 2 + MOD_EPSILON)
        mod_coef = to_harm(first_mod.reshape(PAIRS * DIRS, NPHI, NTHETA), True).reshape(PAIRS, DIRS, 2, L, L)
        second_coef = jnp.einsum('pl,drs,pdqls->pdrqls', kap_second, eta_slots, mod_coef, precision=HIGHEST_PREC)
        second_maps = to_grid(second_coef.reshape(PAIRS * DIRS * 2, 2, L, L), False).reshape(PAIRS, DIRS, 2, NPHI, NTHETA)
        second_mod = jnp.sqrt(second_maps[:, :, 0] ** 2 + second_maps[:, :, 1] ** 2 + MOD_EPSILON)
        cov = lax.optimization_barrier(jnp.sum(cycle_weight * pair_mod * second_mod, axis=(2, 3))) / (NTHETA * NPHI)
        return 0.5 * jnp.sum((cov - target) ** 2)
    value, pullback = jax.vjp(objective, grid_field)
    return pullback(jnp.ones_like(value))[0] * (NTHETA * NPHI)
```

```python
import functools
import math

import jax
import jax.numpy as jnp
from jax import lax
from jax.experimental import pallas as pl
from jax.experimental.pallas import tpu as pltpu
from jax.sharding import PartitionSpec as P

F32 = jnp.float32
BF16 = jnp.bfloat16
HIGHEST_PREC = lax.Precision.HIGHEST
MOD_EPSILON = 0.01
L = 720
NPHI = 1440
NTHETA = 768
LAT = 8
ORD = 16
SLOT = 45
SP = 48
SA = ORD * SP
LP = 768
KP = 768
SB = 8
STEPS = SP // SB
COV_ROW = SLOT
COV_STEP, COV_SUB = COV_ROW // SB, COV_ROW % SB
KT = 256
NORMING = math.sqrt(2.0 / NPHI)
VMEM = 50 * 1024 * 1024


def params(**kw):
    return pltpu.CompilerParams(vmem_limit_bytes=VMEM, **kw)


def lane_low(shape):
    return lax.broadcasted_iota(jnp.int32, shape, len(shape) - 1) % 128 < 64


def swap(x):
    return pltpu.roll(x, 64, x.ndim - 1)


def halves(first, second):
    low = lane_low(first.shape)
    return jnp.where(low, first, swap(second)), jnp.where(low, swap(first), second)


def split_rows(x):
    high = x.astype(BF16).astype(F32)
    return jnp.concatenate([high, x - high], axis=0).astype(BF16)


def dot(a, b):
    return lax.dot_general(a, b, (((1,), (0,)), ((), ())), preferred_element_type=F32)


def dot_t(a, b):
    return lax.dot_general(a, b, (((1,), (1,)), ((), ())), preferred_element_type=F32)


def analysis_one(x_ref, w_ref, m_ref, out_ref):
    w = w_ref[...]
    for s in range(SB):
        rows = x_ref[:, s, :] * w
        d = dot(split_rows(rows), m_ref[s])
        out_ref[:, s, :] = d[:2] + d[2:]


def analysis_fields(carry, x_ref, w_ref, m_ref, out_ref):
    w = w_ref[...]
    for s in range(SB):
        rows = x_ref[:, s, :]
        q0, q1 = halves(rows[:8], rows[8:])
        d = dot(split_rows(jnp.concatenate([q0 * w, q1 * w], axis=0)), m_ref[s])
        out_ref[0, s] = d[0:8] + d[16:24]
        out_ref[1, s] = d[8:16] + d[24:32]
    if carry:

        @pl.when(pl.program_id(0) == COV_STEP)
        def _():
            rows = x_ref[:, COV_SUB, :]
            total = (rows[:8] + rows[8:])[:, 0:1]
            out_ref[0, COV_SUB] = jnp.broadcast_to(total, (8, LP))


def analysis_sum(x_ref, kap_ref, m_ref, out_ref):
    kap = kap_ref[...]
    for s in range(SB):
        parts = []
        for w in range(2):
            rows = x_ref[:, w, s, :]
            parts += list(halves(rows[:8], rows[8:]))
        d = dot(split_rows(jnp.concatenate(parts, axis=0)), m_ref[s])
        d = d[:32] + d[32:]
        for q in range(2):
            both = d[8 * q : 8 * q + 8] * kap[0] + d[16 + 8 * q : 24 + 8 * q] * kap[1]
            out_ref[q, pl.ds(s, 1), :] = jnp.sum(both, axis=0, keepdims=True)


def in_order(core_ref, mine, other):
    even = core_ref[0] == 0
    return jnp.where(even, mine, other), jnp.where(even, other, mine)


def synthesis_first(core_ref, mine_ref, other_ref, kap_ref, m_ref, out_ref):
    kap = kap_ref[...]
    for s in range(SB):
        b0, b1 = in_order(core_ref, mine_ref[pl.ds(s, 1), :], other_ref[pl.ds(s, 1), :])
        rows = jnp.concatenate([kap[0] * b0, kap[0] * b1, kap[1] * b0, kap[1] * b1], axis=0)
        d = dot_t(split_rows(rows), m_ref[s])
        d = d[:32] + d[32:]
        for w in range(2):
            h0, h1 = halves(d[16 * w : 16 * w + 8], d[16 * w + 8 : 16 * w + 16])
            out_ref[:, w, s, :] = jnp.concatenate([h0, h1], axis=0)


def synthesis_fields(
    carry, core_ref, mine_ref, other_ref, kap_ref, w_ref, m_ref, mcov_ref, ocov_ref, target_ref, out_ref
):
    kap = kap_ref[...]
    w = w_ref[...]
    if carry:
        cov, _ = in_order(core_ref, mcov_ref[COV_SUB][:, 0:1], ocov_ref[COV_SUB][:, 0:1])
        residual = cov / (NTHETA * NPHI) - target_ref[...]
        kap = kap * residual
    for s in range(SB):
        b0, b1 = in_order(core_ref, mine_ref[s], other_ref[s])
        rows = jnp.concatenate([b0 * kap, b1 * kap], axis=0)
        d = dot_t(split_rows(rows), m_ref[s])
        d = (d[:16] + d[16:]) * w
        h0, h1 = halves(d[:8], d[8:])
        out_ref[:, s, :] = jnp.concatenate([h0, h1], axis=0)
    if carry:

        @pl.when(pl.program_id(0) == COV_STEP)
        def _():
            wide = jnp.broadcast_to(residual, (8, 128))
            out_ref[:, COV_SUB, :] = jnp.concatenate([wide, wide], axis=0)


def synthesis_last(core_ref, mine_ref, other_ref, w_ref, m_ref, out_ref):
    w = w_ref[...]
    for s in range(SB):
        b0, b1 = in_order(core_ref, mine_ref[pl.ds(s, 1), :], other_ref[pl.ds(s, 1), :])
        d = dot_t(split_rows(jnp.concatenate([b0, b1], axis=0)), m_ref[s])
        out_ref[:, s, :] = (d[:2] + d[2:]) * w


SMEM_SPEC = pl.BlockSpec(memory_space=pltpu.SMEM)


def whole(*shape):
    return pl.BlockSpec(shape, lambda i: (0,) * len(shape))


M_SPEC = pl.BlockSpec((SB, 128, LP), lambda i: (i, 0, 0))
ROW_SPEC = pl.BlockSpec((SB, LP), lambda i: (i, 0))


def cost(flops, nbytes):
    return pl.CostEstimate(flops=int(flops), bytes_accessed=int(nbytes), transcendentals=0)


def leg_cost(rows):
    return cost(2 * SP * rows * 128 * LP, SP * 128 * LP * 2 + SP * rows * LP * 2)


def run_analysis_one(x, w, m):
    return pl.pallas_call(
        analysis_one,
        grid=(STEPS,),
        in_specs=[pl.BlockSpec((2, SB, 128), lambda i: (0, i, 0)), whole(1, 128), M_SPEC],
        out_specs=pl.BlockSpec((2, SB, LP), lambda i: (0, i, 0)),
        out_shape=jax.ShapeDtypeStruct((2, SP, LP), F32),
        compiler_params=params(),
        cost_estimate=leg_cost(4),
        name="analysis_one",
    )(x, w, m)


def run_analysis_fields(x, w, m, carry):
    return pl.pallas_call(
        functools.partial(analysis_fields, carry),
        grid=(STEPS,),
        in_specs=[pl.BlockSpec((16, SB, 128), lambda i: (0, i, 0)), whole(1, 128), M_SPEC],
        out_specs=pl.BlockSpec((2, SB, 8, LP), lambda i: (0, i, 0, 0)),
        out_shape=jax.ShapeDtypeStruct((2, SP, 8, LP), F32),
        compiler_params=params(),
        cost_estimate=leg_cost(32),
        name="analysis_fields",
    )(x, w, m)


def run_analysis_sum(x, kap, m):
    return pl.pallas_call(
        analysis_sum,
        grid=(STEPS,),
        in_specs=[pl.BlockSpec((16, 2, SB, 128), lambda i: (0, 0, i, 0)), whole(2, 8, LP), M_SPEC],
        out_specs=pl.BlockSpec((2, SB, LP), lambda i: (0, i, 0)),
        out_shape=jax.ShapeDtypeStruct((2, SP, LP), F32),
        compiler_params=params(),
        cost_estimate=leg_cost(64),
        name="analysis_sum",
    )(x, kap, m)


def run_synthesis_first(core, mine, other, kap, m):
    return pl.pallas_call(
        synthesis_first,
        grid=(STEPS,),
        in_specs=[SMEM_SPEC, ROW_SPEC, ROW_SPEC, whole(2, 8, LP), M_SPEC],
        out_specs=pl.BlockSpec((16, 2, SB, 128), lambda i: (0, 0, i, 0)),
        out_shape=jax.ShapeDtypeStruct((16, 2, SP, 128), F32),
        compiler_params=params(),
        cost_estimate=leg_cost(64),
        name="synthesis_first",
    )(core, mine, other, kap, m)


def run_synthesis_fields(core, mine, other, kap, w, m, target, carry):
    field = pl.BlockSpec((SB, 8, LP), lambda i: (i, 0, 0))
    cov = pl.BlockSpec((SB, 8, 128), lambda i: (COV_STEP, 0, 0))
    return pl.pallas_call(
        functools.partial(synthesis_fields, carry),
        grid=(STEPS,),
        in_specs=[SMEM_SPEC, field, field, whole(8, LP), whole(1, 128), M_SPEC, cov, cov, whole(8, 1)],
        out_specs=pl.BlockSpec((16, SB, 128), lambda i: (0, i, 0)),
        out_shape=jax.ShapeDtypeStruct((16, SP, 128), F32),
        compiler_params=params(),
        cost_estimate=leg_cost(32),
        name="synthesis_fields",
    )(core, mine, other, kap, w, m, mine, other, target)


def run_synthesis_last(core, mine, other, w, m):
    return pl.pallas_call(
        synthesis_last,
        grid=(STEPS,),
        in_specs=[SMEM_SPEC, ROW_SPEC, ROW_SPEC, whole(1, 128), M_SPEC],
        out_specs=pl.BlockSpec((2, SB, 128), lambda i: (0, i, 0)),
        out_shape=jax.ShapeDtypeStruct((2, SP, 128), F32),
        compiler_params=params(),
        cost_estimate=leg_cost(4),
        name="synthesis_last",
    )(core, mine, other, w, m)


def store_split(x, high_ref, low_ref):
    high = x.astype(BF16)
    high_ref[...] = high
    low_ref[...] = (x - high.astype(F32)).astype(BF16)


def product(w_high, w_low, x_high, x_low):
    return dot(w_high, x_high) + dot(w_high, x_low) + dot(w_low, x_high)


def forward_step(values, high_w, low_w):
    high = values.astype(BF16)
    low = (values - high.astype(F32)).astype(BF16)
    return product(high_w, low_w, high, low)


def pack_parts(z, eta):
    low = lane_low(z.shape)
    other = swap(z)
    return jnp.where(low, z, other) * eta, jnp.where(low, other, z) * eta


def mod(maps):
    squares = maps * maps
    return jnp.sqrt(squares + swap(squares) + MOD_EPSILON)


def inverse_step(ic, iss, wch, wcl, wsh, wsl):
    even = product(wch[...], wcl[...], ic[0][...], ic[1][...])
    odd = product(wsh[...], wsl[...], iss[0][...], iss[1][...])
    return even + odd, even - odd


def accumulate(yc_ref, ys_ref, up, down, tch, tcl, tsh, tsl):
    c = forward_step(up + down, tch[...], tcl[...])
    s = forward_step(up - down, tsh[...], tsl[...])

    @pl.when(pl.program_id(0) == 0)
    def _():
        yc_ref[...] = c
        ys_ref[...] = s

    @pl.when(pl.program_id(0) > 0)
    def _():
        yc_ref[...] += c
        ys_ref[...] += s


def sum_parts(yc, ys, eta):
    vc, vs = yc * eta, ys * eta
    return jnp.where(lane_low(vc.shape), vc + swap(vc), vs + swap(vs))


def is_last():
    return pl.program_id(0) == pl.num_programs(0) - 1


def longitude_first(
    z_ref, eta_ref, wch, wcl, wsh, wsl, tch, tcl, tsh, tsl,
    out_ref, first_ref, pair_ref, ch, cl, sh, sl, yc, ys,
):
    @pl.when(pl.program_id(0) == 0)
    def _():
        eta = eta_ref[...]
        cs, ss = [], []
        for w in range(2):
            c, s = pack_parts(z_ref[:, w].reshape(SA, 128), eta)
            cs.append(c)
            ss.append(s)
        store_split(jnp.concatenate(cs, axis=1), ch, cl)
        store_split(jnp.concatenate(ss, axis=1), sh, sl)

    up, down = inverse_step((ch, cl), (sh, sl), wch, wcl, wsh, wsl)
    first_ref[0] = up[:, :128]
    first_ref[1] = down[:, :128]
    pair_ref[0] = up[:, 128:]
    pair_ref[1] = down[:, 128:]
    accumulate(yc, ys, mod(up[:, :128]), mod(down[:, :128]), tch, tcl, tsh, tsl)

    @pl.when(is_last())
    def _():
        out_ref[...] = jnp.where(lane_low((SA, 128)), yc[...], ys[...]).reshape(ORD, SP, 128)


def longitude_second(
    z_ref, eta_ref, weight_ref, fold_ref, pair_ref, wch, wcl, wsh, wsl, tch, tcl, tsh, tsl,
    out_ref, ratio_ref, ch, cl, sh, sl, yc, ys, cov,
):
    @pl.when(pl.program_id(0) == 0)
    def _():
        c, s = pack_parts(z_ref[...].reshape(SA, 128), eta_ref[...])
        store_split(c, ch, cl)
        store_split(s, sh, sl)
        cov[...] = jnp.zeros_like(cov)

    maps = inverse_step((ch, cl), (sh, sl), wch, wcl, wsh, wsl)
    weight = weight_ref[...]
    grads = []
    total = 0.0
    for i in range(2):
        second_mod = mod(maps[i])
        pair_mod = mod(pair_ref[i])
        total += pair_mod * second_mod
        grads.append(maps[i] * (weight * pair_mod / second_mod))
        ratio_ref[i] = pair_ref[i] * (weight * second_mod / pair_mod)
    cov[...] += jnp.sum(total * fold_ref[...], axis=0, keepdims=True) * weight
    accumulate(yc, ys, grads[0], grads[1], tch, tcl, tsh, tsl)

    @pl.when(is_last())
    def _():
        out = sum_parts(yc[...], ys[...], eta_ref[...]).reshape(ORD, SP, 128)
        lanes = lax.broadcasted_iota(jnp.int32, (1, 128), 1)
        value = jnp.sum(jnp.where(lanes < 64, cov[...], 0.0), axis=1, keepdims=True)
        rows = lax.broadcasted_iota(jnp.int32, (1, SP, 128), 1)
        out_ref[...] = jnp.where(rows == COV_ROW, value.reshape(1, 1, 1), out)


def longitude_third(
    z_ref, eta_ref, first_ref, ratio_ref, wch, wcl, wsh, wsl, tch, tcl, tsh, tsl,
    out_ref, ch, cl, sh, sl, yc, ys,
):
    @pl.when(pl.program_id(0) == 0)
    def _():
        c, s = pack_parts(z_ref[...].reshape(SA, 128), 1.0)
        store_split(c, ch, cl)
        store_split(s, sh, sl)

    maps = inverse_step((ch, cl), (sh, sl), wch, wcl, wsh, wsl)
    residual = z_ref[0, pl.ds(COV_ROW, 1), 0:1]
    grads = []
    for i in range(2):
        first = first_ref[i]
        grads.append(
            jnp.concatenate([first * (maps[i] / mod(first)), ratio_ref[i] * residual], axis=1)
        )
    accumulate(yc, ys, grads[0], grads[1], tch, tcl, tsh, tsl)

    @pl.when(is_last())
    def _():
        eta = eta_ref[...]
        for w in range(2):
            part = slice(128 * w, 128 * w + 128)
            out_ref[:, w] = sum_parts(yc[:, part], ys[:, part], eta).reshape(ORD, SP, 128)


W_SPEC = pl.BlockSpec((KT, SA), lambda i: (i, 0))
T_SPEC = pl.BlockSpec((SA, KT), lambda i: (0, i))
MAP_SPEC = pl.BlockSpec((2, KT, 128), lambda i: (0, i, 0))
MAP_SHAPE = jax.ShapeDtypeStruct((2, KP, 128), F32)


def lon_scratch(n_in, n_out):
    return [pltpu.VMEM((SA, n_in), BF16)] * 4 + [pltpu.VMEM((SA, n_out), F32)] * 2


def lon_cost(n_in, n_out):
    return cost(12 * KP * SA * (n_in + n_out), 8 * KP * SA * 2 + 3 * KP * 128 * 4)


def run_longitude_first(z, eta, waves):
    return pl.pallas_call(
        longitude_first,
        grid=(KP // KT,),
        in_specs=[whole(ORD, 2, SP, 128), whole(SA, 128)] + [W_SPEC] * 4 + [T_SPEC] * 4,
        out_specs=[whole(ORD, SP, 128), MAP_SPEC, MAP_SPEC],
        out_shape=[jax.ShapeDtypeStruct((ORD, SP, 128), F32), MAP_SHAPE, MAP_SHAPE],
        scratch_shapes=lon_scratch(256, 128),
        compiler_params=params(),
        cost_estimate=lon_cost(256, 128),
        name="longitude_first",
    )(z, eta, *waves)


def run_longitude_second(z, eta, weight, fold, pair, waves):
    return pl.pallas_call(
        longitude_second,
        grid=(KP // KT,),
        in_specs=[
            whole(ORD, SP, 128), whole(SA, 128), whole(1, 128),
            pl.BlockSpec((KT, 128), lambda i: (i, 0)), MAP_SPEC,
        ]
        + [W_SPEC] * 4
        + [T_SPEC] * 4,
        out_specs=[whole(ORD, SP, 128), MAP_SPEC],
        out_shape=[jax.ShapeDtypeStruct((ORD, SP, 128), F32), MAP_SHAPE],
        scratch_shapes=lon_scratch(128, 128) + [pltpu.VMEM((1, 128), F32)],
        compiler_params=params(),
        cost_estimate=lon_cost(128, 128),
        name="longitude_second",
    )(z, eta, weight, fold, pair, *waves)


def run_longitude_third(z, eta, first, ratio, waves):
    return pl.pallas_call(
        longitude_third,
        grid=(KP // KT,),
        in_specs=[whole(ORD, SP, 128), whole(SA, 128), MAP_SPEC, MAP_SPEC]
        + [W_SPEC] * 4
        + [T_SPEC] * 4,
        out_specs=whole(ORD, 2, SP, 128),
        out_shape=jax.ShapeDtypeStruct((ORD, 2, SP, 128), F32),
        scratch_shapes=lon_scratch(128, 256),
        compiler_params=params(),
        cost_estimate=lon_cost(128, 256),
        name="longitude_third",
    )(z, eta, first, ratio, *waves)


def split_array(x):
    high = lax.reduce_precision(x, 8, 7)
    return high.astype(BF16), (x - high).astype(BF16)


def angle(product_of):
    return (product_of % NPHI).astype(F32) * (2.0 * math.pi / NPHI)


def make_waves(slots, valid):
    scale = jnp.where(valid, NORMING, 0.0).astype(F32)
    coarse = jnp.arange(KP // 32, dtype=jnp.int32)[:, None] * 32 * slots[None, :]
    fine = jnp.arange(32, dtype=jnp.int32)[:, None] * slots[None, :]
    ca, sa = jnp.cos(angle(coarse)) * scale, jnp.sin(angle(coarse)) * scale
    cb, sb = jnp.cos(angle(fine)), jnp.sin(angle(fine))
    ca, sa, cb, sb = lax.optimization_barrier((ca, sa, cb, sb))
    keep = (jnp.arange(KP) <= NPHI // 2)[:, None]
    wc = jnp.where(keep, (ca[:, None] * cb[None] - sa[:, None] * sb[None]).reshape(KP, SA), 0.0)
    ws = jnp.where(keep, (sa[:, None] * cb[None] + ca[:, None] * sb[None]).reshape(KP, SA), 0.0)
    coarse = jnp.arange(KP // 128, dtype=jnp.int32)[None, :] * 128 * slots[:, None]
    fine = jnp.arange(128, dtype=jnp.int32)[None, :] * slots[:, None]
    ca, sa = jnp.cos(angle(coarse)) * scale[:, None], jnp.sin(angle(coarse)) * scale[:, None]
    cb, sb = jnp.cos(angle(fine)), jnp.sin(angle(fine))
    ca, sa, cb, sb = lax.optimization_barrier((ca, sa, cb, sb))
    fold = fold_weights()[None, :]
    tc = jnp.concatenate([ca[:, i : i + 1] * cb - sa[:, i : i + 1] * sb for i in range(KP // 128)], axis=1)
    ts = jnp.concatenate([sa[:, i : i + 1] * cb + ca[:, i : i + 1] * sb for i in range(KP // 128)], axis=1)
    arrays = []
    for table in (wc, ws, tc * fold, ts * fold):
        arrays += list(split_array(table))
    return lax.optimization_barrier(tuple(arrays))


def fold_weights():
    k = jnp.arange(KP)
    half = NPHI // 2
    return jnp.where((k == 0) | (k == half), 0.5, jnp.where(k < half, 1.0, 0.0)).astype(F32)


def pad_cycles(x):
    lead = x.shape[:-1]
    x = x.reshape(lead + (2, 48))
    return jnp.pad(x, [(0, 0)] * len(lead) + [(0, 0), (0, 16)]).reshape(lead + (128,))


def pad_degrees(x):
    return jnp.pad(x, [(0, 0)] * (x.ndim - 1) + [(0, LP - L)])


def ord_exchange(x):
    return lax.all_to_all(x, "ord", split_axis=0, concat_axis=0, tiled=True)


def ord_gather(x):
    return ord_exchange(jnp.broadcast_to(x[None], (ORD,) + x.shape))


Z_GROUPS = [[0, 2, 4, 6], [1, 3, 5, 7]]


def z_exchange(x):
    return lax.all_to_all(x, "lat", split_axis=0, concat_axis=0, tiled=True, axis_index_groups=Z_GROUPS)


def core_swap(x):
    return lax.ppermute(x, "lat", [(i, i ^ 1) for i in range(LAT)])


def z_shift(x, step):
    return lax.ppermute(x, "lat", [(i, (i + 2 * step) % LAT) for i in range(LAT)])


def core_sum(parts, core):
    mine = lax.dynamic_index_in_dim(parts, core, 0, keepdims=False)
    away = lax.dynamic_index_in_dim(parts, 1 - core, 0, keepdims=False)
    return mine + core_swap(away)


def lat_sum_small(parts, core):
    mine = core_sum(parts, core)
    mine = mine + z_shift(mine, 1) + z_shift(mine, 3) + z_shift(mine, 2)
    return mine, core_swap(mine)


def lat_sum_large(parts, core):
    mine = core_sum(parts, core)
    blocks = z_exchange(mine.reshape(4, SP // 4, 8, LP))
    block = blocks[0] + blocks[1] + blocks[2] + blocks[3]
    mine = z_exchange(jnp.broadcast_to(block[None], (4,) + block.shape)).reshape(SP, 8, LP)
    return mine, core_swap(mine)


def shards(grid_field, legendre, cycle_weight, slot_order, kappa, eta, pairs, target):
    me = lax.axis_index("ord")
    core = lax.axis_index("lat") % 2
    core_flag = core.astype(jnp.int32).reshape(1)
    direction = me % 4

    field = jnp.pad(pad_cycles(grid_field), [(0, 6), (0, 0)])
    field_all = ord_gather(field).reshape(ORD * 96, 128)

    slots2 = jnp.pad(slot_order.reshape(ORD, SLOT), [(0, 0), (0, SP - SLOT)])
    valid2 = jnp.broadcast_to(jnp.arange(SP) < SLOT, (ORD, SP))
    slots, valid = slots2.reshape(SA), valid2.reshape(SA)
    my_slots = lax.dynamic_index_in_dim(slots2, me, 0, keepdims=False)
    own_valid = jnp.arange(SP) < SLOT
    degree_ids = jnp.arange(L, dtype=jnp.int32)
    table = jnp.where(degree_ids[None, None, :] >= my_slots[None, :SLOT, None], legendre, jnp.zeros((), BF16))
    table = jnp.transpose(table, (1, 0, 2)).reshape(SLOT, 2, 48, L)
    table = jnp.pad(table, [(0, SP - SLOT), (0, 0), (0, 16), (0, LP - L)]).reshape(SP, 128, LP)

    offset = jnp.arange(96, dtype=jnp.int32)
    longitude = (jnp.arange(ORD, dtype=jnp.int32)[:, None] * 90 + offset[None, :]).reshape(ORD * 96)
    k_valid = jnp.broadcast_to(offset < 90, (ORD, 96)).reshape(ORD * 96)
    phase = angle(my_slots[:, None] * longitude[None, :])
    own_scale = jnp.where(own_valid[:, None] & k_valid[None, :], NORMING, 0.0).astype(F32)
    own_waves = jnp.stack([jnp.cos(phase) * own_scale, jnp.sin(phase) * own_scale]).reshape(2 * SP, ORD * 96)

    phase = angle((me * 90 + offset)[:, None] * slots[None, :])
    end_scale = jnp.where(valid[None, :], NORMING, 0.0).astype(F32)
    end_waves = jnp.stack(
        [(jnp.cos(phase) * end_scale).reshape(96, ORD, SP), (jnp.sin(phase) * end_scale).reshape(96, ORD, SP)], axis=2
    ).reshape(96, ORD * 2 * SP)

    waves = make_waves(slots, valid)
    eta_rows = lax.dynamic_index_in_dim(eta, direction, 0, keepdims=False)
    hit = slots[:, None] == degree_ids[None, :]
    eta_cols = [jnp.sum(jnp.where(hit, eta_rows[r][None, :], 0.0), axis=1, keepdims=True) for r in range(2)]
    eta_lanes = jnp.where(jnp.arange(128)[None, :] < 64, eta_cols[0], eta_cols[1])

    scale_ids = jnp.arange(kappa.shape[0], dtype=jnp.int32)
    picks = [(pairs[:, i : i + 1] == scale_ids[None, :]).astype(F32) for i in range(2)]
    kaps = [pad_degrees(jnp.sum(pick[:, :, None] * kappa[None], axis=1)) for pick in picks]
    kap_rows = jnp.stack([jnp.repeat(kap, 4, axis=0) for kap in kaps])
    kap_second = kap_rows[1]
    target_rows = target.reshape(8, 1)

    weight_lanes = pad_cycles(cycle_weight[None, :])
    ones = jnp.ones((1, 128), F32)
    weight_halves = weight_lanes.reshape(2, 64)
    my_weight = lax.dynamic_index_in_dim(weight_halves, me // 8, 0, keepdims=True)
    my_weight = jnp.concatenate([my_weight, my_weight], axis=1)
    fold_lanes = jnp.broadcast_to(fold_weights()[:, None], (KP, 128))

    spectra = jnp.dot(own_waves, field_all, precision=HIGHEST_PREC).reshape(2, SP, 128)
    mine, other = lat_sum_small(run_analysis_one(spectra, weight_lanes, table), core)
    z_first = ord_exchange(run_synthesis_first(core_flag, mine, other, kap_rows, table))
    spectra, first_maps, pair_maps = run_longitude_first(z_first, eta_lanes, waves)
    parts = run_analysis_fields(ord_exchange(spectra), weight_lanes, table, False)
    mine, other = lat_sum_large(parts, core)
    z_second = ord_exchange(
        run_synthesis_fields(core_flag, mine, other, kap_second, ones, table, target_rows, False)
    )
    spectra, ratio = run_longitude_second(z_second, eta_lanes, my_weight, fold_lanes, pair_maps, waves)
    parts = run_analysis_fields(ord_exchange(spectra), ones, table, True)
    mine, other = lat_sum_large(parts, core)
    z_third = ord_exchange(
        run_synthesis_fields(core_flag, mine, other, kap_second, weight_lanes, table, target_rows, True)
    )
    spectra = run_longitude_third(z_third, eta_lanes, first_maps, ratio, waves)
    mine, other = lat_sum_small(run_analysis_sum(ord_exchange(spectra), kap_rows, table), core)
    cycles = run_synthesis_last(core_flag, mine, other, weight_lanes, table)
    cycles_all = ord_gather(cycles.reshape(2 * SP, 128)).reshape(ORD * 2 * SP, 128)
    result = jnp.dot(end_waves, cycles_all, precision=HIGHEST_PREC)
    return result[:90].reshape(90, 2, 64)[:, :, :48].reshape(90, 96)


def solution(mesh):
    return jax.shard_map(
        shards,
        mesh=mesh,
        in_specs=(P("ord", "lat"), P("lat", "ord", None), P("lat"), P(), P(), P(), P(), P()),
        out_specs=P("ord", "lat"),
        check_vma=False,
    )
```

```python
import functools
import math

import jax
import jax.numpy as jnp
from jax import lax
from jax.experimental import pallas as pl
from jax.experimental.pallas import tpu as pltpu
from jax.sharding import PartitionSpec as P

F32 = jnp.float32
BF16 = jnp.bfloat16
HIGHEST_PREC = lax.Precision.HIGHEST
MOD_EPSILON = 0.01
L = 720
NPHI = 1440
NTHETA = 768
LAT = 8
ORD = 16
SLOT = 45
SP = 48
SA = ORD * SP
LP = 768
KP = 768
SB = 8
STEPS = SP // SB
HALF = STEPS // 2
ZB = SP // 4
KT = 256
NORMING = math.sqrt(2.0 / NPHI)
VMEM = 16 * 1024 * 1024
LON_VMEM = 54 * 1024 * 1024


def params(limit=VMEM):
    return pltpu.CompilerParams(vmem_limit_bytes=limit)


def lane_low(shape):
    return lax.broadcasted_iota(jnp.int32, shape, len(shape) - 1) % 128 < 64


def swap(x):
    return pltpu.roll(x, 64, x.ndim - 1)


def halves(first, second):
    low = lane_low(first.shape)
    return jnp.where(low, first, swap(second)), jnp.where(low, swap(first), second)


def split_rows(x):
    high = x.astype(BF16).astype(F32)
    return jnp.concatenate([high, x - high], axis=0).astype(BF16)


def dot(a, b):
    return lax.dot_general(a, b, (((1,), (0,)), ((), ())), preferred_element_type=F32)


def dot_t(a, b):
    return lax.dot_general(a, b, (((1,), (1,)), ((), ())), preferred_element_type=F32)


def compact(x):
    low = lax.broadcasted_iota(jnp.int32, x.shape, 1) < 48
    return jnp.where(low, x, pltpu.roll(x, 112, 1))[:, :96]


def expand(y):
    y = jnp.concatenate([y, jnp.zeros((y.shape[0], 32), F32)], axis=1)
    low = lax.broadcasted_iota(jnp.int32, y.shape, 1) < 48
    return jnp.where(low, y, pltpu.roll(y, 16, 1))


def quad_index(step, part, z):
    quad = 2 * step + part
    return lax.rem(z + lax.div(quad, 3), 4) * 3 + lax.rem(quad, 3)


def slot_tables(first_step, info_ref, tables):
    step = pl.program_id(0) + first_step
    for s in range(SB):
        yield s, (tables[s // 4].at[s % 4], info_ref[2 + step * SB + s])


def degree_mask(rows, order):
    return lax.broadcasted_iota(jnp.int32, (rows, L), 1) >= order


def forward_rows(rows, entry):
    table, order = entry
    n = rows.shape[0]
    d = dot(split_rows(compact(rows)), table[...])
    return jnp.where(degree_mask(n, order), d[:n] + d[n:], 0.0)


def backward_rows(rows, entry):
    table, order = entry
    n = rows.shape[0]
    d = dot_t(split_rows(jnp.where(degree_mask(n, order), rows[:, :L], 0.0)), table[...])
    return expand(jnp.where(order < L, d[:n] + d[n:], 0.0))


def analysis_one(info_ref, x_ref, w_ref, m0, m1, out_ref):
    w = w_ref[...]
    for s, table in slot_tables(0, info_ref, (m0, m1)):
        out_ref[:, s, 0:L] = forward_rows(x_ref[:, s, :] * w, table)
        out_ref[:, s, L:] = jnp.zeros((2, LP - L), F32)


def analysis_fields(first_step, carry, info_ref, x_ref, w_ref, m0, m1, out_ref):
    w = w_ref[...]
    for s, table in slot_tables(first_step, info_ref, (m0, m1)):
        rows = x_ref[:, s, :]
        q0, q1 = halves(rows[:8], rows[8:])
        d = forward_rows(jnp.concatenate([q0 * w, q1 * w], axis=0), table)
        out_ref[0, s, :, 0:L] = d[:8]
        out_ref[1, s, :, 0:L] = d[8:]
        rest = jnp.zeros((8, LP - L), F32)
        out_ref[1, s, :, L:] = rest
        if carry:
            rest = jnp.broadcast_to((rows[:8] + rows[8:])[:, 48:49], (8, LP - L))
        out_ref[0, s, :, L:] = rest


def analysis_sum(info_ref, x_ref, kap_ref, m0, m1, out_ref):
    kap = kap_ref[:, :, :L]
    for s, table in slot_tables(0, info_ref, (m0, m1)):
        parts = []
        for w in range(2):
            rows = x_ref[:, w, s, :]
            parts += list(halves(rows[:8], rows[8:]))
        d = forward_rows(jnp.concatenate(parts, axis=0), table)
        for q in range(2):
            both = d[8 * q : 8 * q + 8] * kap[0] + d[16 + 8 * q : 24 + 8 * q] * kap[1]
            out_ref[q, pl.ds(s, 1), 0:L] = jnp.sum(both, axis=0, keepdims=True)
            out_ref[q, pl.ds(s, 1), L:] = jnp.zeros((1, LP - L), F32)


def in_order(info_ref, mine, other):
    even = info_ref[1] == 0
    return jnp.where(even, mine, other), jnp.where(even, other, mine)


def residual_of(info_ref, mcov_ref, ocov_ref, target_ref):
    lane = L - (LP - 128)
    cov, _ = in_order(info_ref, mcov_ref[0][:, lane : lane + 1], ocov_ref[0][:, lane : lane + 1])
    return cov / (NTHETA * NPHI) - target_ref[...]


def both_halves(d, extra=None):
    h0, h1 = halves(d[:8], d[8:])
    out = jnp.concatenate([h0, h1], axis=0)
    if extra is not None:
        lanes = lax.broadcasted_iota(jnp.int32, out.shape, 1) % 64
        out = jnp.where(lanes >= 48, jnp.concatenate([extra, extra], axis=0), out)
    return out


def synthesis_base(info_ref, mine_ref, other_ref, kap_ref, m0, m1, out_ref):
    kap = kap_ref[...]
    for s, table in slot_tables(0, info_ref, (m0, m1)):
        b0, b1 = in_order(info_ref, mine_ref[pl.ds(s, 1), :], other_ref[pl.ds(s, 1), :])
        rows = jnp.concatenate([kap[0] * b0, kap[0] * b1, kap[1] * b0, kap[1] * b1], axis=0)
        d = backward_rows(rows, table)
        for w in range(2):
            out_ref[:, w, s, :] = both_halves(d[16 * w : 16 * w + 16])


def synthesis_fields(first_step, carry, info_ref, mine_ref, other_ref, kap_ref, w_ref, mcov_ref, ocov_ref, target_ref, m0, m1, *refs):
    out_ref = refs[-1]
    kap = kap_ref[...]
    w = w_ref[...]
    residual = None
    if carry:
        residual = residual_of(info_ref, mcov_ref, ocov_ref, target_ref)
        kap = kap * residual
    for s, table in slot_tables(first_step, info_ref, (m0, m1)):
        b0, b1 = in_order(info_ref, mine_ref[s], other_ref[s])
        d = backward_rows(jnp.concatenate([b0 * kap, b1 * kap], axis=0), table) * w
        out_ref[:, s, :] = both_halves(d, residual)


def synthesis_last(info_ref, mine_ref, other_ref, w_ref, m0, m1, out_ref):
    w = w_ref[...]
    for s, table in slot_tables(0, info_ref, (m0, m1)):
        b0, b1 = in_order(info_ref, mine_ref[pl.ds(s, 1), :], other_ref[pl.ds(s, 1), :])
        out_ref[:, s, :] = backward_rows(jnp.concatenate([b0, b1], axis=0), table) * w


def whole(*shape):
    return pl.BlockSpec(shape, lambda i, *_: (0,) * len(shape))


ROW_SPEC = pl.BlockSpec((SB, LP), lambda i, *_: (i, 0))
PLANE_SPEC = pl.BlockSpec((2, SB, LP), lambda i, *_: (0, i, 0))
COV_SPEC = pl.BlockSpec((1, 8, 128), lambda i, *_: (0, 0, LP // 128 - 1))
PLANE_SHAPE = jax.ShapeDtypeStruct((2, SP, LP), F32)
SENT_PAIR_SHAPE = jax.ShapeDtypeStruct((ORD, 2, SP, 128), F32)
SENT_SHAPE = jax.ShapeDtypeStruct((ORD, SP, 128), F32)


def table_specs(first_step):
    def spec(part):
        return pl.BlockSpec((4, 96, L), lambda i, info: (quad_index(i + first_step, part, info[0]), 0, 0))

    return [spec(0), spec(1)]


def sent_spec(first_step=0):
    return pl.BlockSpec((ORD, SB, 128), lambda i, *_: (0, i + first_step, 0))


def sent_pair_spec():
    return pl.BlockSpec((ORD, 2, SB, 128), lambda i, *_: (0, 0, i, 0))


def cost(flops, nbytes):
    return pl.CostEstimate(flops=int(flops), bytes_accessed=int(nbytes), transcendentals=0)


def leg_call(kernel, steps, first_step, specs, out_spec, out_shape, rows, name, aliases=None, extra=()):
    n = steps * SB
    return pl.pallas_call(
        kernel,
        grid_spec=pltpu.PrefetchScalarGridSpec(
            num_scalar_prefetch=1,
            grid=(steps,),
            in_specs=specs + table_specs(first_step) + list(extra),
            out_specs=out_spec,
        ),
        out_shape=out_shape,
        input_output_aliases=aliases or {},
        compiler_params=params(),
        cost_estimate=cost(2 * n * rows * 128 * LP, n * 96 * LP * 2 + n * rows * LP * 2),
        name=name,
    )


def run_analysis_one(info, x, w, m):
    specs = [pl.BlockSpec((2, SB, 128), lambda i, *_: (0, i, 0)), whole(1, 128)]
    return leg_call(analysis_one, STEPS, 0, specs, PLANE_SPEC, PLANE_SHAPE, 4, "analysis_one")(info, x, w, m, m)


def run_analysis_fields(info, x, w, m, first_step, steps, carry):
    specs = [sent_spec(first_step), whole(1, 128)]
    return leg_call(
        functools.partial(analysis_fields, first_step, carry), steps, first_step, specs,
        pl.BlockSpec((2, SB, 8, LP), lambda i, *_: (0, i, 0, 0)),
        jax.ShapeDtypeStruct((2, steps * SB, 8, LP), F32), 32, "analysis_fields",
    )(info, x, w, m, m)


def run_analysis_sum(info, x, kap, m):
    specs = [sent_pair_spec(), whole(2, 8, LP)]
    return leg_call(analysis_sum, STEPS, 0, specs, PLANE_SPEC, PLANE_SHAPE, 64, "analysis_sum")(info, x, kap, m, m)


def run_synthesis_base(info, mine, other, kap, m):
    specs = [ROW_SPEC, ROW_SPEC, whole(2, 8, LP)]
    return leg_call(
        synthesis_base, STEPS, 0, specs, sent_pair_spec(), SENT_PAIR_SHAPE, 64, "synthesis_base"
    )(info, mine, other, kap, m, m)


def run_synthesis_fields(info, fields, kap, w, m, target, carry):
    out = None
    field = pl.BlockSpec((SB, 8, LP), lambda i, *_: (i, 0, 0))
    specs = [field, field, whole(8, LP), whole(1, 128), COV_SPEC, COV_SPEC, whole(8, 1)]
    mcov, ocov = fields[0]
    for (first_step, steps), (mine, other) in zip(((0, HALF), (HALF, HALF)), fields):
        operands = [info, mine, other, kap, w, mcov, ocov, target, m, m]
        aliases, extra = None, ()
        if out is not None:
            aliases, extra = {len(operands): 0}, (pl.BlockSpec(memory_space=pl.ANY),)
            operands.append(out)
        out = leg_call(
            functools.partial(synthesis_fields, first_step, carry), steps, first_step, specs,
            sent_spec(first_step), SENT_SHAPE, 32, "synthesis_fields", aliases, extra,
        )(*operands)
    return out


def run_synthesis_last(info, mine, other, w, m):
    specs = [ROW_SPEC, ROW_SPEC, whole(1, 128)]
    return leg_call(
        synthesis_last, STEPS, 0, specs, pl.BlockSpec((2, SB, 128), lambda i, *_: (0, i, 0)),
        jax.ShapeDtypeStruct((2, SP, 128), F32), 4, "synthesis_last",
    )(info, mine, other, w, m, m)


def store_split(x, high_ref, low_ref):
    high = x.astype(BF16)
    high_ref[...] = high
    low_ref[...] = (x - high.astype(F32)).astype(BF16)


def product(w_high, w_low, x_high, x_low):
    n = x_high.shape[1]
    if n > 128:
        return dot(w_high, x_high) + dot(w_high, x_low) + dot(w_low, x_high)
    both = dot(w_high, jnp.concatenate([x_high, x_low], axis=1))
    return both[:, :n] + both[:, n:] + dot(w_low, x_high)


def forward_step(values, high_w, low_w):
    high = values.astype(BF16)
    low = (values - high.astype(F32)).astype(BF16)
    return product(high_w, low_w, high, low)


def pack_parts(z, eta):
    low = lane_low(z.shape)
    other = swap(z)
    return jnp.where(low, z, other) * eta, jnp.where(low, other, z) * eta


def mod(maps):
    squares = maps * maps
    return jnp.sqrt(squares + swap(squares) + MOD_EPSILON)


def inverse_step(ic, iss, w_ref):
    even = product(w_ref[0], w_ref[1], ic[0][...], ic[1][...])
    odd = product(w_ref[2], w_ref[3], iss[0][...], iss[1][...])
    return even + odd, even - odd


def accumulate(yc_ref, ys_ref, up, down, t_ref):
    c = forward_step(up + down, t_ref[0], t_ref[1])
    s = forward_step(up - down, t_ref[2], t_ref[3])

    @pl.when(pl.program_id(0) == 0)
    def _():
        yc_ref[...] = c
        ys_ref[...] = s

    @pl.when(pl.program_id(0) > 0)
    def _():
        yc_ref[...] += c
        ys_ref[...] += s


def sum_parts(yc, ys, eta):
    vc, vs = yc * eta, ys * eta
    return jnp.where(lane_low(vc.shape), vc + swap(vc), vs + swap(vs))


def is_last():
    return pl.program_id(0) == pl.num_programs(0) - 1


def start_inverse(z_ref, eta, ch, cl, sh, sl):
    @pl.when(pl.program_id(0) == 0)
    def _():
        c, s = pack_parts(z_ref[...].reshape(SA, 128), eta)
        store_split(c, ch, cl)
        store_split(s, sh, sl)


def longitude_first(
    z_ref, eta_ref, w_ref, t_ref, out_ref, first_ref, pair_ref, ch, cl, sh, sl, yc, ys,
):
    @pl.when(pl.program_id(0) == 0)
    def _():
        eta = eta_ref[...]
        parts = [pack_parts(z_ref[:, w].reshape(SA, 128), eta) for w in range(2)]
        store_split(jnp.concatenate([parts[0][0], parts[1][0]], axis=1), ch, cl)
        store_split(jnp.concatenate([parts[0][1], parts[1][1]], axis=1), sh, sl)

    maps = inverse_step((ch, cl), (sh, sl), w_ref)
    for i in range(2):
        first_ref[i] = maps[i][:, :128]
        pair_ref[i] = maps[i][:, 128:]
    accumulate(yc, ys, mod(maps[0][:, :128]), mod(maps[1][:, :128]), t_ref)

    @pl.when(is_last())
    def _():
        out_ref[...] = jnp.where(lane_low((SA, 128)), yc[...], ys[...]).reshape(ORD, SP, 128)


def longitude_second(
    z_ref, eta_ref, weight_ref, fold_ref, pair_ref, w_ref, t_ref,
    out_ref, ratio_ref, ch, cl, sh, sl, yc, ys, cov,
):
    start_inverse(z_ref, eta_ref[...], ch, cl, sh, sl)

    @pl.when(pl.program_id(0) == 0)
    def _():
        cov[...] = jnp.zeros_like(cov)

    maps = inverse_step((ch, cl), (sh, sl), w_ref)
    weight = weight_ref[...]
    grads = []
    total = 0.0
    for i in range(2):
        second_mod = mod(maps[i])
        pair_mod = mod(pair_ref[i])
        total += pair_mod * second_mod
        grads.append(maps[i] * (weight * pair_mod / second_mod))
        ratio_ref[i] = pair_ref[i] * (weight * second_mod / pair_mod)
    cov[...] += jnp.sum(total * fold_ref[...], axis=0, keepdims=True) * weight
    accumulate(yc, ys, grads[0], grads[1], t_ref)

    @pl.when(is_last())
    def _():
        lanes = lax.broadcasted_iota(jnp.int32, (1, 128), 1)
        value = jnp.sum(jnp.where(lanes < 48, cov[...], 0.0), axis=1, keepdims=True)
        out = sum_parts(yc[...], ys[...], eta_ref[...])
        lanes = lax.broadcasted_iota(jnp.int32, (SA, 128), 1) % 64
        out_ref[...] = jnp.where(lanes >= 48, value, out).reshape(ORD, SP, 128)


def longitude_third(
    z_ref, eta_ref, first_ref, ratio_ref, w_ref, t_ref, out_ref, ch, cl, sh, sl, yc, ys,
):
    start_inverse(z_ref, 1.0, ch, cl, sh, sl)
    maps = inverse_step((ch, cl), (sh, sl), w_ref)
    residual = z_ref[0, 0:1, 48:49]
    grads = []
    for i in range(2):
        first = first_ref[i]
        grads.append(jnp.concatenate([first * (maps[i] / mod(first)), ratio_ref[i] * residual], axis=1))
    accumulate(yc, ys, grads[0], grads[1], t_ref)

    @pl.when(is_last())
    def _():
        eta = eta_ref[...]
        for w in range(2):
            part = slice(128 * w, 128 * w + 128)
            out_ref[:, w] = sum_parts(yc[:, part], ys[:, part], eta).reshape(ORD, SP, 128)


W_SPEC = pl.BlockSpec((4, KT, SA), lambda i: (0, i, 0))
T_SPEC = pl.BlockSpec((4, SA, KT), lambda i: (0, 0, i))
MAP_SPEC = pl.BlockSpec((2, KT, 128), lambda i: (0, i, 0))
MAP_SHAPE = jax.ShapeDtypeStruct((2, KP, 128), F32)


def lon_scratch(n_in, n_out):
    return [pltpu.VMEM((SA, n_in), BF16)] * 4 + [pltpu.VMEM((SA, n_out), F32)] * 2


def lon_call(kernel, specs, outs, scratch, name):
    n = len(scratch) // 2
    return pl.pallas_call(
        kernel,
        grid=(KP // KT,),
        in_specs=specs,
        out_specs=[o[0] for o in outs],
        out_shape=[o[1] for o in outs],
        scratch_shapes=scratch,
        compiler_params=params(LON_VMEM),
        cost_estimate=cost(6 * n * KP * SA * 128, 4 * KP * SA * 2 + 3 * KP * 128 * 4),
        name=name,
    )


SENT_PAIR = (whole(ORD, 2, SP, 128), SENT_PAIR_SHAPE)
SENT = (whole(ORD, SP, 128), SENT_SHAPE)
MAPS = (MAP_SPEC, MAP_SHAPE)
LANES = whole(SA, 128)


def run_longitude_first(z, eta, waves):
    specs = [SENT_PAIR[0], LANES] + [W_SPEC, T_SPEC]
    return lon_call(longitude_first, specs, [SENT, MAPS, MAPS], lon_scratch(256, 128), "longitude_first")(
        z, eta, *waves
    )


def run_longitude_second(z, eta, weight, fold, pair, waves):
    fold_spec = pl.BlockSpec((KT, 128), lambda i: (i, 0))
    specs = [SENT[0], LANES, whole(1, 128), fold_spec, MAP_SPEC] + [W_SPEC, T_SPEC]
    scratch = lon_scratch(128, 128) + [pltpu.VMEM((1, 128), F32)]
    return lon_call(longitude_second, specs, [SENT, MAPS], scratch, "longitude_second")(
        z, eta, weight, fold, pair, *waves
    )


def run_longitude_third(z, eta, first, ratio, waves):
    specs = [SENT[0], LANES, MAP_SPEC, MAP_SPEC] + [W_SPEC, T_SPEC]
    return lon_call(longitude_third, specs, [SENT_PAIR], lon_scratch(128, 256), "longitude_third")(
        z, eta, first, ratio, *waves
    )[0]


def angle(product_of):
    return (product_of % NPHI).astype(F32) * (2.0 * math.pi / NPHI)


def wave_tables(slots, valid):
    scale = jnp.where(valid, NORMING, 0.0).astype(F32)
    tables = []
    for step, count in ((32, KP // 32), (1, 32)):
        phase = angle(jnp.arange(count, dtype=jnp.int32)[:, None] * step * slots[None, :])
        tables.append(jnp.stack([jnp.cos(phase), jnp.sin(phase)]) * (scale[None, None, :] if step > 1 else 1.0))
    for step in (128, 1):
        phase = angle(jnp.arange(128, dtype=jnp.int32)[None, :] * step * slots[:, None])
        tables.append(jnp.stack([jnp.cos(phase), jnp.sin(phase)]) * (scale[None, :, None] if step > 1 else 1.0))
    return tables


def fill_waves(coarse_ref, fine_ref, tcoarse_ref, tfine_ref, w_ref, t_ref):
    i = pl.program_id(0)
    cb, sb = fine_ref[0], fine_ref[1]
    for j in range(4):
        ca, sa = [coarse_ref[part, pl.ds(4 * i + j, 1), :] for part in range(2)]
        k = lax.broadcasted_iota(jnp.int32, (32, SA), 0) + (128 * i + 32 * j)
        keep = k <= NPHI // 2
        rows = pl.ds(32 * j, 32)
        for value, high, low in ((ca * cb - sa * sb, 0, 1), (sa * cb + ca * sb, 2, 3)):
            value = jnp.where(keep, value, 0.0)
            head = value.astype(BF16)
            w_ref[high, rows, :] = head
            w_ref[low, rows, :] = (value - head.astype(F32)).astype(BF16)
    cb, sb = tfine_ref[0], tfine_ref[1]
    for j in range(KP // 128):
        ca, sa = tcoarse_ref[0][:, j : j + 1], tcoarse_ref[1][:, j : j + 1]
        k = lax.broadcasted_iota(jnp.int32, (1, 128), 1) + 128 * j
        fold = jnp.where((k == 0) | (k == NPHI // 2), 0.5, jnp.where(k < NPHI // 2, 1.0, 0.0))
        cols = pl.ds(128 * j, 128)
        for value, high, low in ((ca * cb - sa * sb, 0, 1), (sa * cb + ca * sb, 2, 3)):
            value = value * fold
            head = value.astype(BF16)
            t_ref[high, :, cols] = head
            t_ref[low, :, cols] = (value - head.astype(F32)).astype(BF16)


def make_waves(tables):
    slot_rows = pl.BlockSpec((2, 128, 128), lambda i: (0, i, 0))
    return pl.pallas_call(
        fill_waves,
        grid=(KP // 128,),
        in_specs=[whole(2, KP // 32, SA), whole(2, 32, SA), slot_rows, slot_rows],
        out_specs=[pl.BlockSpec((4, 128, SA), lambda i: (0, i, 0))] * 2,
        out_shape=[pltpu.HBM((4, KP, SA), BF16)] * 2,
        compiler_params=params(),
        cost_estimate=cost(32 * KP * SA, 16 * KP * SA),
        name="fill_waves",
    )(*tables)


def fold_weights():
    k = jnp.arange(KP)
    half = NPHI // 2
    return jnp.where((k == 0) | (k == half), 0.5, jnp.where(k < half, 1.0, 0.0)).astype(F32)


def pad_cycles(x):
    lead = x.shape[:-1]
    x = x.reshape(lead + (2, 48))
    return jnp.pad(x, [(0, 0)] * len(lead) + [(0, 0), (0, 16)]).reshape(lead + (128,))


def pad_degrees(x):
    return jnp.pad(x, [(0, 0)] * (x.ndim - 1) + [(0, LP - L)])


def ord_exchange(x):
    return lax.all_to_all(x, "ord", split_axis=0, concat_axis=0, tiled=True)


def ord_gather(x):
    return ord_exchange(jnp.broadcast_to(x[None], (ORD,) + x.shape))


def core_swap(x):
    return lax.ppermute(x, "lat", [(i, i ^ 1) for i in range(LAT)])


def z_shift(x, step):
    return lax.ppermute(x, "lat", [(i, (i + 2 * step) % LAT) for i in range(LAT)])


def core_sum(parts, core):
    mine = lax.dynamic_index_in_dim(parts, core, 0, keepdims=False)
    away = lax.dynamic_index_in_dim(parts, 1 - core, 0, keepdims=False)
    return mine + core_swap(away)


def turn_blocks(x, count):
    return jnp.concatenate([x[count * ZB :], x[: count * ZB]], axis=0)


def lat_sum_small(parts, core):
    mine = core_sum(parts, core)
    there = [z_shift(mine, step) for step in range(1, 4)]
    total = mine
    for step in range(1, 4):
        total = total + turn_blocks(there[step - 1], step)
    return total, core_swap(total)


def lat_sum_large(high, low, core):
    high = core_sum(high, core)
    there = z_shift(high[:ZB], 2), z_shift(high[ZB:], 3)
    low = core_sum(low, core)
    own = low[:ZB] + there[0] + z_shift(low[ZB:], 1) + there[1]
    blocks = [own, z_shift(own, 3), z_shift(own, 2), z_shift(own, 1)]
    others = [core_swap(x) for x in blocks]
    return [
        (jnp.concatenate(blocks[i : i + 2], axis=0), jnp.concatenate(others[i : i + 2], axis=0)) for i in (0, 2)
    ]


def after(x, *done):
    return lax.optimization_barrier((x,) + done)[0]


def shards(grid_field, legendre, cycle_weight, slot_order, kappa, eta, pairs, target):
    me = lax.axis_index("ord")
    z, core = lax.axis_index("lat") // 2, lax.axis_index("lat") % 2
    info = jnp.stack([z, core]).astype(jnp.int32)
    direction = me % 4

    field = jnp.pad(pad_cycles(grid_field), [(0, 6), (0, 0)])
    field_all = ord_gather(field).reshape(ORD * 96, 128)

    position = jnp.arange(SP, dtype=jnp.int32)
    quad = quad_index(position // SB, position // 4 % 2, z)
    place = quad * 4 + position % 4
    slots2 = jnp.pad(slot_order.reshape(ORD, SLOT), [(0, 0), (0, SP - SLOT)])
    slots2 = jnp.sum(jnp.where(place[None, :, None] == position[None, None, :], slots2[:, None, :], 0), axis=2)
    own_valid = place < SLOT
    slots = slots2.reshape(SA)
    valid = jnp.broadcast_to(own_valid, (ORD, SP)).reshape(SA)
    my_slots = lax.dynamic_index_in_dim(slots2, me, 0, keepdims=False)
    degree_ids = jnp.arange(L, dtype=jnp.int32)
    info = jnp.concatenate([info, jnp.where(own_valid, my_slots, L)])
    table = jnp.transpose(legendre, (1, 0, 2))

    offset = jnp.arange(96, dtype=jnp.int32)
    longitude = (jnp.arange(ORD, dtype=jnp.int32)[:, None] * 90 + offset[None, :]).reshape(ORD * 96)
    k_valid = jnp.broadcast_to(offset < 90, (ORD, 96)).reshape(ORD * 96)
    phase = angle(my_slots[:, None] * longitude[None, :])
    own_scale = jnp.where(own_valid[:, None] & k_valid[None, :], NORMING, 0.0).astype(F32)
    own_waves = jnp.stack([jnp.cos(phase) * own_scale, jnp.sin(phase) * own_scale]).reshape(2 * SP, ORD * 96)

    weight_lanes = pad_cycles(cycle_weight[None, :])
    spectra = jnp.dot(own_waves, field_all, precision=HIGHEST_PREC).reshape(2, SP, 128)
    parts = run_analysis_one(info, spectra, weight_lanes, table)

    eta_rows = lax.dynamic_index_in_dim(eta, direction, 0, keepdims=False)
    hit = slots[:, None] == degree_ids[None, :]
    eta_cols = [jnp.sum(jnp.where(hit, eta_rows[r][None, :], 0.0), axis=1, keepdims=True) for r in range(2)]
    eta_lanes = jnp.where(jnp.arange(128)[None, :] < 64, eta_cols[0], eta_cols[1])

    scale_ids = jnp.arange(kappa.shape[0], dtype=jnp.int32)
    picks = [(pairs[:, i : i + 1] == scale_ids[None, :]).astype(F32) for i in range(2)]
    kaps = [pad_degrees(jnp.sum(pick[:, :, None] * kappa[None], axis=1)) for pick in picks]
    kap_rows = jnp.stack([jnp.repeat(kap, 4, axis=0) for kap in kaps])
    kap_second = kap_rows[1]
    target_rows = target.reshape(8, 1)
    ones = jnp.ones((1, 128), F32)
    my_weight = lax.dynamic_index_in_dim(weight_lanes.reshape(2, 64), me // 8, 0, keepdims=True)
    my_weight = jnp.concatenate([my_weight, my_weight], axis=1)
    fold_lanes = jnp.broadcast_to(fold_weights()[:, None], (KP, 128))

    def all_sums(x, w, carry):
        high = run_analysis_fields(info, x, w, table, HALF, HALF, carry)
        low = run_analysis_fields(info, x, after(w, high), table, 0, HALF, carry)
        return lat_sum_large(high, low, core)

    mine, other = lat_sum_small(parts, core)
    cycles = run_synthesis_base(info, mine, other, kap_rows, table)
    z_first = ord_exchange(cycles)
    waves = make_waves(after(wave_tables(slots, valid), cycles))
    spectra, first_maps, pair_maps = run_longitude_first(z_first, eta_lanes, waves)
    sums = all_sums(ord_exchange(spectra), weight_lanes, False)
    z_second = ord_exchange(run_synthesis_fields(info, sums, kap_second, ones, table, target_rows, False))
    spectra, ratio = run_longitude_second(z_second, eta_lanes, my_weight, fold_lanes, pair_maps, waves)
    sums = all_sums(ord_exchange(spectra), ones, True)
    z_third = ord_exchange(run_synthesis_fields(info, sums, kap_second, weight_lanes, table, target_rows, True))
    spectra = run_longitude_third(z_third, eta_lanes, first_maps, ratio, waves)
    mine, other = lat_sum_small(run_analysis_sum(info, ord_exchange(spectra), kap_rows, table), core)
    cycles = run_synthesis_last(info, mine, other, weight_lanes, table)

    end_slots = after(slots, z_third)
    phase = angle((me * 90 + offset)[:, None] * end_slots[None, :])
    end_scale = jnp.where(valid[None, :], NORMING, 0.0).astype(F32)
    end_waves = jnp.stack(
        [(jnp.cos(phase) * end_scale).reshape(96, ORD, SP), (jnp.sin(phase) * end_scale).reshape(96, ORD, SP)], axis=2
    ).reshape(96, ORD * 2 * SP)
    cycles_all = ord_gather(cycles.reshape(2 * SP, 128)).reshape(ORD * 2 * SP, 128)
    result = jnp.dot(end_waves, cycles_all, precision=HIGHEST_PREC)
    return result[:90].reshape(90, 2, 64)[:, :, :48].reshape(90, 96)


def solution(mesh):
    return jax.shard_map(
        shards,
        mesh=mesh,
        in_specs=(P("ord", "lat"), P("lat", "ord", None), P("lat"), P(), P(), P(), P(), P()),
        out_specs=P("ord", "lat"),
        check_vma=False,
    )
```

```python
import functools
import math

import jax
import jax.numpy as jnp
from jax import lax
from jax.experimental import pallas as pl
from jax.experimental.pallas import tpu as pltpu
from jax.sharding import PartitionSpec as P

F32 = jnp.float32
BF16 = jnp.bfloat16
HIGHEST_PREC = lax.Precision.HIGHEST
MOD_EPSILON = 0.01
L = 720
NPHI = 1440
NTHETA = 768
LAT = 8
ORD = 16
SLOT = 45
SP = 48
SA = ORD * SP
LP = 768
KP = 768
SB = 8
STEPS = SP // SB
HALF = STEPS // 2
ZB = SP // 4
KT = 384
NORMING = math.sqrt(2.0 / NPHI)
VMEM = 16 * 1024 * 1024
LON_VMEM = 54 * 1024 * 1024


def params(limit=VMEM):
    return pltpu.CompilerParams(vmem_limit_bytes=limit)


def lane_low(shape):
    return lax.broadcasted_iota(jnp.int32, shape, len(shape) - 1) % 128 < 64


def swap(x):
    return pltpu.roll(x, 64, x.ndim - 1)


def halves(first, second):
    low = lane_low(first.shape)
    return jnp.where(low, first, swap(second)), jnp.where(low, swap(first), second)


def split_rows(x):
    high = x.astype(BF16).astype(F32)
    return jnp.concatenate([high, x - high], axis=0).astype(BF16)


def dot(a, b):
    return lax.dot_general(a, b, (((1,), (0,)), ((), ())), preferred_element_type=F32)


def dot_t(a, b):
    return lax.dot_general(a, b, (((1,), (1,)), ((), ())), preferred_element_type=F32)


def compact(x):
    low = lax.broadcasted_iota(jnp.int32, x.shape, 1) < 48
    return jnp.where(low, x, pltpu.roll(x, 112, 1))[:, :96]


def expand(y):
    y = jnp.concatenate([y, jnp.zeros((y.shape[0], 32), F32)], axis=1)
    low = lax.broadcasted_iota(jnp.int32, y.shape, 1) < 48
    return jnp.where(low, y, pltpu.roll(y, 16, 1))


def quad_index(step, part, z):
    quad = 2 * step + part
    return lax.rem(z + lax.div(quad, 3), 4) * 3 + lax.rem(quad, 3)


def slot_tables(first_step, info_ref, tables):
    step = pl.program_id(0) + first_step
    for s in range(SB):
        yield s, (tables[s // 4].at[s % 4], info_ref[2 + step * SB + s])


def degree_mask(rows, order):
    return lax.broadcasted_iota(jnp.int32, (rows, L), 1) >= order


def forward_rows(rows, entry):
    table, order = entry
    n = rows.shape[0]
    d = dot(split_rows(compact(rows)), table[...])
    return jnp.where(degree_mask(n, order), d[:n] + d[n:], 0.0)


def backward_rows(rows, entry):
    table, order = entry
    n = rows.shape[0]
    d = dot_t(split_rows(jnp.where(degree_mask(n, order), rows[:, :L], 0.0)), table[...])
    return expand(jnp.where(order < L, d[:n] + d[n:], 0.0))


def analysis_one(info_ref, x_ref, w_ref, m0, m1, out_ref):
    w = w_ref[...]
    for s, table in slot_tables(0, info_ref, (m0, m1)):
        out_ref[:, s, 0:L] = forward_rows(x_ref[:, s, :] * w, table)
        out_ref[:, s, L:] = jnp.zeros((2, LP - L), F32)


def analysis_fields(first_step, carry, info_ref, x_ref, w_ref, m0, m1, out_ref):
    w = w_ref[...]
    for s, table in slot_tables(first_step, info_ref, (m0, m1)):
        rows = x_ref[:, s, :]
        q0, q1 = halves(rows[:8], rows[8:])
        d = forward_rows(jnp.concatenate([q0 * w, q1 * w], axis=0), table)
        out_ref[0, s, :, 0:L] = d[:8]
        out_ref[1, s, :, 0:L] = d[8:]
        rest = jnp.zeros((8, LP - L), F32)
        out_ref[1, s, :, L:] = rest
        if carry:
            rest = jnp.broadcast_to((rows[:8] + rows[8:])[:, 48:49], (8, LP - L))
        out_ref[0, s, :, L:] = rest


def analysis_sum(info_ref, x_ref, kap_ref, m0, m1, out_ref):
    kap = kap_ref[:, :, :L]
    for s, table in slot_tables(0, info_ref, (m0, m1)):
        parts = []
        for w in range(2):
            rows = x_ref[:, w, s, :]
            parts += list(halves(rows[:8], rows[8:]))
        d = forward_rows(jnp.concatenate(parts, axis=0), table)
        for q in range(2):
            both = d[8 * q : 8 * q + 8] * kap[0] + d[16 + 8 * q : 24 + 8 * q] * kap[1]
            out_ref[q, pl.ds(s, 1), 0:L] = jnp.sum(both, axis=0, keepdims=True)
            out_ref[q, pl.ds(s, 1), L:] = jnp.zeros((1, LP - L), F32)


def in_order(info_ref, mine, other):
    even = info_ref[1] == 0
    return jnp.where(even, mine, other), jnp.where(even, other, mine)


def residual_of(info_ref, mcov_ref, ocov_ref, target_ref):
    lane = L - (LP - 128)
    cov, _ = in_order(info_ref, mcov_ref[0][:, lane : lane + 1], ocov_ref[0][:, lane : lane + 1])
    return cov / (NTHETA * NPHI) - target_ref[...]


def both_halves(d, extra=None):
    h0, h1 = halves(d[:8], d[8:])
    out = jnp.concatenate([h0, h1], axis=0)
    if extra is not None:
        lanes = lax.broadcasted_iota(jnp.int32, out.shape, 1) % 64
        out = jnp.where(lanes >= 48, jnp.concatenate([extra, extra], axis=0), out)
    return out


def synthesis_base(info_ref, mine_ref, other_ref, kap_ref, m0, m1, out_ref):
    kap = kap_ref[...]
    for s, table in slot_tables(0, info_ref, (m0, m1)):
        b0, b1 = in_order(info_ref, mine_ref[pl.ds(s, 1), :], other_ref[pl.ds(s, 1), :])
        rows = jnp.concatenate([kap[0] * b0, kap[0] * b1, kap[1] * b0, kap[1] * b1], axis=0)
        d = backward_rows(rows, table)
        for w in range(2):
            out_ref[:, w, s, :] = both_halves(d[16 * w : 16 * w + 16])


def synthesis_fields(first_step, carry, info_ref, mine_ref, other_ref, kap_ref, w_ref, mcov_ref, ocov_ref, target_ref, m0, m1, *refs):
    out_ref = refs[-1]
    kap = kap_ref[...]
    w = w_ref[...]
    residual = None
    if carry:
        residual = residual_of(info_ref, mcov_ref, ocov_ref, target_ref)
        kap = kap * residual
    for s, table in slot_tables(first_step, info_ref, (m0, m1)):
        b0, b1 = in_order(info_ref, mine_ref[s], other_ref[s])
        d = backward_rows(jnp.concatenate([b0 * kap, b1 * kap], axis=0), table) * w
        out_ref[:, s, :] = both_halves(d, residual)


def synthesis_last(info_ref, mine_ref, other_ref, w_ref, m0, m1, out_ref):
    w = w_ref[...]
    for s, table in slot_tables(0, info_ref, (m0, m1)):
        b0, b1 = in_order(info_ref, mine_ref[pl.ds(s, 1), :], other_ref[pl.ds(s, 1), :])
        out_ref[:, s, :] = backward_rows(jnp.concatenate([b0, b1], axis=0), table) * w


def whole(*shape):
    return pl.BlockSpec(shape, lambda i, *_: (0,) * len(shape))


ROW_SPEC = pl.BlockSpec((SB, LP), lambda i, *_: (i, 0))
PLANE_SPEC = pl.BlockSpec((2, SB, LP), lambda i, *_: (0, i, 0))
COV_SPEC = pl.BlockSpec((1, 8, 128), lambda i, *_: (0, 0, LP // 128 - 1))
PLANE_SHAPE = jax.ShapeDtypeStruct((2, SP, LP), F32)
SENT_PAIR_SHAPE = jax.ShapeDtypeStruct((ORD, 2, SP, 128), F32)
SENT_SHAPE = jax.ShapeDtypeStruct((ORD, SP, 128), F32)


def table_specs(first_step):
    def spec(part):
        return pl.BlockSpec((4, 96, L), lambda i, info: (quad_index(i + first_step, part, info[0]), 0, 0))

    return [spec(0), spec(1)]


def sent_spec(first_step=0):
    return pl.BlockSpec((ORD, SB, 128), lambda i, *_: (0, i + first_step, 0))


def sent_pair_spec():
    return pl.BlockSpec((ORD, 2, SB, 128), lambda i, *_: (0, 0, i, 0))


def cost(flops, nbytes):
    return pl.CostEstimate(flops=int(flops), bytes_accessed=int(nbytes), transcendentals=0)


def leg_call(kernel, steps, first_step, specs, out_spec, out_shape, rows, name, aliases=None, extra=()):
    n = steps * SB
    return pl.pallas_call(
        kernel,
        grid_spec=pltpu.PrefetchScalarGridSpec(
            num_scalar_prefetch=1,
            grid=(steps,),
            in_specs=specs + table_specs(first_step) + list(extra),
            out_specs=out_spec,
        ),
        out_shape=out_shape,
        input_output_aliases=aliases or {},
        compiler_params=params(),
        cost_estimate=cost(2 * n * rows * 128 * LP, n * 96 * LP * 2 + n * rows * LP * 2),
        name=name,
    )


def run_analysis_one(info, x, w, m):
    specs = [pl.BlockSpec((2, SB, 128), lambda i, *_: (0, i, 0)), whole(1, 128)]
    return leg_call(analysis_one, STEPS, 0, specs, PLANE_SPEC, PLANE_SHAPE, 4, "analysis_one")(info, x, w, m, m)


def run_analysis_fields(info, x, w, m, first_step, steps, carry):
    specs = [sent_spec(first_step), whole(1, 128)]
    return leg_call(
        functools.partial(analysis_fields, first_step, carry), steps, first_step, specs,
        pl.BlockSpec((2, SB, 8, LP), lambda i, *_: (0, i, 0, 0)),
        jax.ShapeDtypeStruct((2, steps * SB, 8, LP), F32), 32, "analysis_fields",
    )(info, x, w, m, m)


def run_analysis_sum(info, x, kap, m):
    specs = [sent_pair_spec(), whole(2, 8, LP)]
    return leg_call(analysis_sum, STEPS, 0, specs, PLANE_SPEC, PLANE_SHAPE, 64, "analysis_sum")(info, x, kap, m, m)


def run_synthesis_base(info, mine, other, kap, m):
    specs = [ROW_SPEC, ROW_SPEC, whole(2, 8, LP)]
    return leg_call(
        synthesis_base, STEPS, 0, specs, sent_pair_spec(), SENT_PAIR_SHAPE, 64, "synthesis_base"
    )(info, mine, other, kap, m, m)


def run_synthesis_fields(info, fields, kap, w, m, target, carry):
    out = None
    field = pl.BlockSpec((SB, 8, LP), lambda i, *_: (i, 0, 0))
    specs = [field, field, whole(8, LP), whole(1, 128), COV_SPEC, COV_SPEC, whole(8, 1)]
    mcov, ocov = fields[0]
    for (first_step, steps), (mine, other) in zip(((0, HALF), (HALF, HALF)), fields):
        operands = [info, mine, other, kap, w, mcov, ocov, target, m, m]
        aliases, extra = None, ()
        if out is not None:
            aliases, extra = {len(operands): 0}, (pl.BlockSpec(memory_space=pl.ANY),)
            operands.append(out)
        out = leg_call(
            functools.partial(synthesis_fields, first_step, carry), steps, first_step, specs,
            sent_spec(first_step), SENT_SHAPE, 32, "synthesis_fields", aliases, extra,
        )(*operands)
    return out


def run_synthesis_last(info, mine, other, w, m):
    specs = [ROW_SPEC, ROW_SPEC, whole(1, 128)]
    return leg_call(
        synthesis_last, STEPS, 0, specs, pl.BlockSpec((2, SB, 128), lambda i, *_: (0, i, 0)),
        jax.ShapeDtypeStruct((2, SP, 128), F32), 4, "synthesis_last",
    )(info, mine, other, w, m, m)


def store_split(x, high_ref, low_ref):
    high = x.astype(BF16)
    high_ref[...] = high
    low_ref[...] = (x - high.astype(F32)).astype(BF16)


def product(w_high, w_low, x_high, x_low):
    n = x_high.shape[1]
    if n > 128:
        return dot(w_high, x_high) + dot(w_high, x_low) + dot(w_low, x_high)
    both = dot(w_high, jnp.concatenate([x_high, x_low], axis=1))
    return both[:, :n] + both[:, n:] + dot(w_low, x_high)


def forward_step(values, high_w, low_w):
    high = values.astype(BF16)
    low = (values - high.astype(F32)).astype(BF16)
    return product(high_w, low_w, high, low)


def pack_parts(z, eta):
    low = lane_low(z.shape)
    other = swap(z)
    return jnp.where(low, z, other) * eta, jnp.where(low, other, z) * eta


def mod(maps):
    squares = maps * maps
    return jnp.sqrt(squares + swap(squares) + MOD_EPSILON)


def inverse_step(ic, iss, w_ref):
    even = product(w_ref[0], w_ref[1], ic[0][...], ic[1][...])
    odd = product(w_ref[2], w_ref[3], iss[0][...], iss[1][...])
    return even + odd, even - odd


def accumulate(yc_ref, ys_ref, up, down, t_ref):
    c = forward_step(up + down, t_ref[0], t_ref[1])
    s = forward_step(up - down, t_ref[2], t_ref[3])

    @pl.when(pl.program_id(0) == 0)
    def _():
        yc_ref[...] = c
        ys_ref[...] = s

    @pl.when(pl.program_id(0) > 0)
    def _():
        yc_ref[...] += c
        ys_ref[...] += s


def sum_parts(yc, ys, eta):
    vc, vs = yc * eta, ys * eta
    return jnp.where(lane_low(vc.shape), vc + swap(vc), vs + swap(vs))


def is_last():
    return pl.program_id(0) == pl.num_programs(0) - 1


def start_inverse(z_ref, eta, ch, cl, sh, sl):
    @pl.when(pl.program_id(0) == 0)
    def _():
        c, s = pack_parts(z_ref[...].reshape(SA, 128), eta)
        store_split(c, ch, cl)
        store_split(s, sh, sl)


def longitude_first(
    z_ref, eta_ref, w_ref, t_ref, out_ref, first_ref, pair_ref, ch, cl, sh, sl, yc, ys,
):
    @pl.when(pl.program_id(0) == 0)
    def _():
        eta = eta_ref[...]
        parts = [pack_parts(z_ref[:, w].reshape(SA, 128), eta) for w in range(2)]
        store_split(jnp.concatenate([parts[0][0], parts[1][0]], axis=1), ch, cl)
        store_split(jnp.concatenate([parts[0][1], parts[1][1]], axis=1), sh, sl)

    maps = inverse_step((ch, cl), (sh, sl), w_ref)
    for i in range(2):
        first_ref[i] = maps[i][:, :128]
        pair_ref[i] = maps[i][:, 128:]
    accumulate(yc, ys, mod(maps[0][:, :128]), mod(maps[1][:, :128]), t_ref)

    @pl.when(is_last())
    def _():
        out_ref[...] = jnp.where(lane_low((SA, 128)), yc[...], ys[...]).reshape(ORD, SP, 128)


def longitude_second(
    z_ref, eta_ref, weight_ref, fold_ref, pair_ref, w_ref, t_ref,
    out_ref, ratio_ref, ch, cl, sh, sl, yc, ys, cov,
):
    start_inverse(z_ref, eta_ref[...], ch, cl, sh, sl)

    @pl.when(pl.program_id(0) == 0)
    def _():
        cov[...] = jnp.zeros_like(cov)

    maps = inverse_step((ch, cl), (sh, sl), w_ref)
    weight = weight_ref[...]
    grads = []
    total = 0.0
    for i in range(2):
        second_mod = mod(maps[i])
        pair_mod = mod(pair_ref[i])
        total += pair_mod * second_mod
        grads.append(maps[i] * (weight * pair_mod / second_mod))
        ratio_ref[i] = pair_ref[i] * (weight * second_mod / pair_mod)
    cov[...] += jnp.sum(total * fold_ref[...], axis=0, keepdims=True) * weight
    accumulate(yc, ys, grads[0], grads[1], t_ref)

    @pl.when(is_last())
    def _():
        lanes = lax.broadcasted_iota(jnp.int32, (1, 128), 1)
        value = jnp.sum(jnp.where(lanes < 48, cov[...], 0.0), axis=1, keepdims=True)
        out = sum_parts(yc[...], ys[...], eta_ref[...])
        lanes = lax.broadcasted_iota(jnp.int32, (SA, 128), 1) % 64
        out_ref[...] = jnp.where(lanes >= 48, value, out).reshape(ORD, SP, 128)


def longitude_third(
    z_ref, eta_ref, first_ref, ratio_ref, w_ref, t_ref, out_ref, ch, cl, sh, sl, yc, ys,
):
    start_inverse(z_ref, 1.0, ch, cl, sh, sl)
    maps = inverse_step((ch, cl), (sh, sl), w_ref)
    residual = z_ref[0, 0:1, 48:49]
    grads = []
    for i in range(2):
        first = first_ref[i]
        grads.append(jnp.concatenate([first * (maps[i] / mod(first)), ratio_ref[i] * residual], axis=1))
    accumulate(yc, ys, grads[0], grads[1], t_ref)

    @pl.when(is_last())
    def _():
        eta = eta_ref[...]
        for w in range(2):
            part = slice(128 * w, 128 * w + 128)
            out_ref[:, w] = sum_parts(yc[:, part], ys[:, part], eta).reshape(ORD, SP, 128)


W_SPEC = pl.BlockSpec((4, KT, SA), lambda i: (0, i, 0))
T_SPEC = pl.BlockSpec((4, SA, KT), lambda i: (0, 0, i))
MAP_SPEC = pl.BlockSpec((2, KT, 128), lambda i: (0, i, 0))
MAP_SHAPE = jax.ShapeDtypeStruct((2, KP, 128), F32)


def lon_scratch(n_in, n_out):
    return [pltpu.VMEM((SA, n_in), BF16)] * 4 + [pltpu.VMEM((SA, n_out), F32)] * 2


def lon_call(kernel, specs, outs, scratch, name):
    n = len(scratch) // 2
    return pl.pallas_call(
        kernel,
        grid=(KP // KT,),
        in_specs=specs,
        out_specs=[o[0] for o in outs],
        out_shape=[o[1] for o in outs],
        scratch_shapes=scratch,
        compiler_params=params(LON_VMEM),
        cost_estimate=cost(6 * n * KP * SA * 128, 4 * KP * SA * 2 + 3 * KP * 128 * 4),
        name=name,
    )


SENT_PAIR = (whole(ORD, 2, SP, 128), SENT_PAIR_SHAPE)
SENT = (whole(ORD, SP, 128), SENT_SHAPE)
MAPS = (MAP_SPEC, MAP_SHAPE)
LANES = whole(SA, 128)


def run_longitude_first(z, eta, waves):
    specs = [SENT_PAIR[0], LANES] + [W_SPEC, T_SPEC]
    return lon_call(longitude_first, specs, [SENT, MAPS, MAPS], lon_scratch(256, 128), "longitude_first")(
        z, eta, *waves
    )


def run_longitude_second(z, eta, weight, fold, pair, waves):
    fold_spec = pl.BlockSpec((KT, 128), lambda i: (i, 0))
    specs = [SENT[0], LANES, whole(1, 128), fold_spec, MAP_SPEC] + [W_SPEC, T_SPEC]
    scratch = lon_scratch(128, 128) + [pltpu.VMEM((1, 128), F32)]
    return lon_call(longitude_second, specs, [SENT, MAPS], scratch, "longitude_second")(
        z, eta, weight, fold, pair, *waves
    )


def run_longitude_third(z, eta, first, ratio, waves):
    specs = [SENT[0], LANES, MAP_SPEC, MAP_SPEC] + [W_SPEC, T_SPEC]
    return lon_call(longitude_third, specs, [SENT_PAIR], lon_scratch(128, 256), "longitude_third")(
        z, eta, first, ratio, *waves
    )[0]


def angle(product_of):
    return (product_of % NPHI).astype(F32) * (2.0 * math.pi / NPHI)


def wave_tables(slots, valid):
    scale = jnp.where(valid, NORMING, 0.0).astype(F32)
    tables = []
    for step, count in ((32, KP // 32), (1, 32)):
        phase = angle(jnp.arange(count, dtype=jnp.int32)[:, None] * step * slots[None, :])
        tables.append(jnp.stack([jnp.cos(phase), jnp.sin(phase)]) * (scale[None, None, :] if step > 1 else 1.0))
    for step in (128, 1):
        phase = angle(jnp.arange(128, dtype=jnp.int32)[None, :] * step * slots[:, None])
        tables.append(jnp.stack([jnp.cos(phase), jnp.sin(phase)]) * (scale[None, :, None] if step > 1 else 1.0))
    return tables


def fill_waves(coarse_ref, fine_ref, tcoarse_ref, tfine_ref, w_ref, t_ref):
    i = pl.program_id(0)
    cb, sb = fine_ref[0], fine_ref[1]
    for j in range(4):
        ca, sa = [coarse_ref[part, pl.ds(4 * i + j, 1), :] for part in range(2)]
        k = lax.broadcasted_iota(jnp.int32, (32, SA), 0) + (128 * i + 32 * j)
        keep = k <= NPHI // 2
        rows = pl.ds(32 * j, 32)
        for value, high, low in ((ca * cb - sa * sb, 0, 1), (sa * cb + ca * sb, 2, 3)):
            value = jnp.where(keep, value, 0.0)
            head = value.astype(BF16)
            w_ref[high, rows, :] = head
            w_ref[low, rows, :] = (value - head.astype(F32)).astype(BF16)
    cb, sb = tfine_ref[0], tfine_ref[1]
    for j in range(KP // 128):
        ca, sa = tcoarse_ref[0][:, j : j + 1], tcoarse_ref[1][:, j : j + 1]
        k = lax.broadcasted_iota(jnp.int32, (1, 128), 1) + 128 * j
        fold = jnp.where((k == 0) | (k == NPHI // 2), 0.5, jnp.where(k < NPHI // 2, 1.0, 0.0))
        cols = pl.ds(128 * j, 128)
        for value, high, low in ((ca * cb - sa * sb, 0, 1), (sa * cb + ca * sb, 2, 3)):
            value = value * fold
            head = value.astype(BF16)
            t_ref[high, :, cols] = head
            t_ref[low, :, cols] = (value - head.astype(F32)).astype(BF16)


def make_waves(tables):
    slot_rows = pl.BlockSpec((2, 128, 128), lambda i: (0, i, 0))
    return pl.pallas_call(
        fill_waves,
        grid=(KP // 128,),
        in_specs=[whole(2, KP // 32, SA), whole(2, 32, SA), slot_rows, slot_rows],
        out_specs=[pl.BlockSpec((4, 128, SA), lambda i: (0, i, 0))] * 2,
        out_shape=[pltpu.HBM((4, KP, SA), BF16)] * 2,
        compiler_params=params(),
        cost_estimate=cost(32 * KP * SA, 16 * KP * SA),
        name="fill_waves",
    )(*tables)


def fold_weights():
    k = jnp.arange(KP)
    half = NPHI // 2
    return jnp.where((k == 0) | (k == half), 0.5, jnp.where(k < half, 1.0, 0.0)).astype(F32)


def pad_cycles(x):
    lead = x.shape[:-1]
    x = x.reshape(lead + (2, 48))
    return jnp.pad(x, [(0, 0)] * len(lead) + [(0, 0), (0, 16)]).reshape(lead + (128,))


def pad_degrees(x):
    return jnp.pad(x, [(0, 0)] * (x.ndim - 1) + [(0, LP - L)])


def ord_exchange(x):
    return lax.all_to_all(x, "ord", split_axis=0, concat_axis=0, tiled=True)


def ord_gather(x):
    return ord_exchange(jnp.broadcast_to(x[None], (ORD,) + x.shape))


def core_swap(x):
    return lax.ppermute(x, "lat", [(i, i ^ 1) for i in range(LAT)])


def z_shift(x, step):
    return lax.ppermute(x, "lat", [(i, (i + 2 * step) % LAT) for i in range(LAT)])


def core_sum(parts, core):
    mine = lax.dynamic_index_in_dim(parts, core, 0, keepdims=False)
    away = lax.dynamic_index_in_dim(parts, 1 - core, 0, keepdims=False)
    return mine + core_swap(away)


def turn_blocks(x, count):
    return jnp.concatenate([x[count * ZB :], x[: count * ZB]], axis=0)


def lat_sum_small(parts, core):
    mine = core_sum(parts, core)
    there = [z_shift(mine, step) for step in range(1, 4)]
    total = mine
    for step in range(1, 4):
        total = total + turn_blocks(there[step - 1], step)
    return total, core_swap(total)


def lat_sum_large(high, low, core):
    high = core_sum(high, core)
    there = z_shift(high[:ZB], 2), z_shift(high[ZB:], 3)
    low = core_sum(low, core)
    own = low[:ZB] + there[0] + z_shift(low[ZB:], 1) + there[1]
    blocks = [own, z_shift(own, 3), z_shift(own, 2), z_shift(own, 1)]
    others = [core_swap(x) for x in blocks]
    return [
        (jnp.concatenate(blocks[i : i + 2], axis=0), jnp.concatenate(others[i : i + 2], axis=0)) for i in (0, 2)
    ]


def after(x, *done):
    return lax.optimization_barrier((x,) + done)[0]


def shards(grid_field, legendre, cycle_weight, slot_order, kappa, eta, pairs, target):
    me = lax.axis_index("ord")
    z, core = lax.axis_index("lat") // 2, lax.axis_index("lat") % 2
    info = jnp.stack([z, core]).astype(jnp.int32)
    direction = me % 4

    field = jnp.pad(pad_cycles(grid_field), [(0, 6), (0, 0)])
    field_all = ord_gather(field).reshape(ORD * 96, 128)

    position = jnp.arange(SP, dtype=jnp.int32)
    quad = quad_index(position // SB, position // 4 % 2, z)
    place = quad * 4 + position % 4
    slots2 = jnp.pad(slot_order.reshape(ORD, SLOT), [(0, 0), (0, SP - SLOT)])
    slots2 = jnp.sum(jnp.where(place[None, :, None] == position[None, None, :], slots2[:, None, :], 0), axis=2)
    own_valid = place < SLOT
    slots = slots2.reshape(SA)
    valid = jnp.broadcast_to(own_valid, (ORD, SP)).reshape(SA)
    my_slots = lax.dynamic_index_in_dim(slots2, me, 0, keepdims=False)
    degree_ids = jnp.arange(L, dtype=jnp.int32)
    info = jnp.concatenate([info, jnp.where(own_valid, my_slots, L)])
    table = jnp.transpose(legendre, (1, 0, 2))

    offset = jnp.arange(96, dtype=jnp.int32)
    longitude = (jnp.arange(ORD, dtype=jnp.int32)[:, None] * 90 + offset[None, :]).reshape(ORD * 96)
    k_valid = jnp.broadcast_to(offset < 90, (ORD, 96)).reshape(ORD * 96)
    phase = angle(my_slots[:, None] * longitude[None, :])
    own_scale = jnp.where(own_valid[:, None] & k_valid[None, :], NORMING, 0.0).astype(F32)
    own_waves = jnp.stack([jnp.cos(phase) * own_scale, jnp.sin(phase) * own_scale]).reshape(2 * SP, ORD * 96)

    weight_lanes = pad_cycles(cycle_weight[None, :])
    own_waves, *tables = lax.optimization_barrier((own_waves, *wave_tables(slots, valid)))
    spectra = jnp.dot(own_waves, field_all, precision=HIGHEST_PREC).reshape(2, SP, 128)
    parts = run_analysis_one(info, spectra, weight_lanes, table)

    eta_rows = lax.dynamic_index_in_dim(eta, direction, 0, keepdims=False)
    hit = slots[:, None] == degree_ids[None, :]
    eta_cols = [jnp.sum(jnp.where(hit, eta_rows[r][None, :], 0.0), axis=1, keepdims=True) for r in range(2)]
    eta_lanes = jnp.where(jnp.arange(128)[None, :] < 64, eta_cols[0], eta_cols[1])

    scale_ids = jnp.arange(kappa.shape[0], dtype=jnp.int32)
    picks = [(pairs[:, i : i + 1] == scale_ids[None, :]).astype(F32) for i in range(2)]
    kaps = [pad_degrees(jnp.sum(pick[:, :, None] * kappa[None], axis=1)) for pick in picks]
    kap_rows = jnp.stack([jnp.repeat(kap, 4, axis=0) for kap in kaps])
    kap_second = kap_rows[1]
    target_rows = target.reshape(8, 1)
    ones = jnp.ones((1, 128), F32)
    my_weight = lax.dynamic_index_in_dim(weight_lanes.reshape(2, 64), me // 8, 0, keepdims=True)
    my_weight = jnp.concatenate([my_weight, my_weight], axis=1)
    fold_lanes = jnp.broadcast_to(fold_weights()[:, None], (KP, 128))

    def all_sums(x, w, carry):
        high = run_analysis_fields(info, x, w, table, HALF, HALF, carry)
        low = run_analysis_fields(info, x, after(w, high), table, 0, HALF, carry)
        return lat_sum_large(high, low, core)

    mine, other = lat_sum_small(parts, core)
    cycles = run_synthesis_base(info, mine, other, kap_rows, table)
    z_first = ord_exchange(cycles)
    waves = make_waves(after(tables, cycles))
    spectra, first_maps, pair_maps = run_longitude_first(z_first, eta_lanes, waves)
    sums = all_sums(ord_exchange(spectra), weight_lanes, False)
    z_second = ord_exchange(run_synthesis_fields(info, sums, kap_second, ones, table, target_rows, False))
    spectra, ratio = run_longitude_second(z_second, eta_lanes, my_weight, fold_lanes, pair_maps, waves)
    sums = all_sums(ord_exchange(spectra), ones, True)
    z_third = ord_exchange(run_synthesis_fields(info, sums, kap_second, weight_lanes, table, target_rows, True))
    spectra = run_longitude_third(z_third, eta_lanes, first_maps, ratio, waves)
    mine, other = lat_sum_small(run_analysis_sum(info, ord_exchange(spectra), kap_rows, table), core)
    cycles = run_synthesis_last(info, mine, other, weight_lanes, table)

    end_slots = after(slots, z_third)
    phase = angle((me * 90 + offset)[:, None] * end_slots[None, :])
    end_scale = jnp.where(valid[None, :], NORMING, 0.0).astype(F32)
    end_waves = jnp.stack(
        [(jnp.cos(phase) * end_scale).reshape(96, ORD, SP), (jnp.sin(phase) * end_scale).reshape(96, ORD, SP)], axis=2
    ).reshape(96, ORD * 2 * SP)
    cycles_all = ord_gather(cycles.reshape(2 * SP, 128)).reshape(ORD * 2 * SP, 128)
    result = jnp.dot(end_waves, cycles_all, precision=HIGHEST_PREC)
    return result[:90].reshape(90, 2, 64)[:, :, :48].reshape(90, 96)


def solution(mesh):
    return jax.shard_map(
        shards,
        mesh=mesh,
        in_specs=(P("ord", "lat"), P("lat", "ord", None), P("lat"), P(), P(), P(), P(), P()),
        out_specs=P("ord", "lat"),
        check_vma=False,
    )
```

```python
import functools
import math

import jax
import jax.numpy as jnp
from jax import lax
from jax.experimental import pallas as pl
from jax.experimental.pallas import tpu as pltpu
from jax.sharding import PartitionSpec as P

F32 = jnp.float32
BF16 = jnp.bfloat16
HIGHEST_PREC = lax.Precision.HIGHEST
MOD_EPSILON = 0.01
L = 720
NPHI = 1440
NTHETA = 768
LAT = 8
ORD = 16
SLOT = 45
SP = 48
SA = ORD * SP
LP = 768
KP = 768
SB = 8
STEPS = SP // SB
HALF = STEPS // 2
ZB = SP // 4
KT = 256
NORMING = math.sqrt(2.0 / NPHI)
VMEM = 16 * 1024 * 1024
LON_VMEM = 54 * 1024 * 1024


def params(limit=VMEM):
    return pltpu.CompilerParams(vmem_limit_bytes=limit)


def lane_low(shape):
    return lax.broadcasted_iota(jnp.int32, shape, len(shape) - 1) % 128 < 64


def swap(x):
    return pltpu.roll(x, 64, x.ndim - 1)


def halves(first, second):
    low = lane_low(first.shape)
    return jnp.where(low, first, swap(second)), jnp.where(low, swap(first), second)


def split_rows(x):
    high = x.astype(BF16).astype(F32)
    return jnp.concatenate([high, x - high], axis=0).astype(BF16)


def dot(a, b):
    return lax.dot_general(a, b, (((1,), (0,)), ((), ())), preferred_element_type=F32)


def dot_t(a, b):
    return lax.dot_general(a, b, (((1,), (1,)), ((), ())), preferred_element_type=F32)


def compact(x):
    low = lax.broadcasted_iota(jnp.int32, x.shape, 1) < 48
    return jnp.where(low, x, pltpu.roll(x, 112, 1))[:, :96]


def expand(y):
    y = jnp.concatenate([y, jnp.zeros((y.shape[0], 32), F32)], axis=1)
    low = lax.broadcasted_iota(jnp.int32, y.shape, 1) < 48
    return jnp.where(low, y, pltpu.roll(y, 16, 1))


def quad_index(step, part, z):
    quad = 2 * step + part
    return lax.rem(z + lax.div(quad, 3), 4) * 3 + lax.rem(quad, 3)


def slot_tables(first_step, info_ref, tables):
    step = pl.program_id(0) + first_step
    for s in range(SB):
        yield s, (tables[s // 4].at[s % 4], info_ref[2 + step * SB + s])


def degree_mask(rows, order):
    return lax.broadcasted_iota(jnp.int32, (rows, L), 1) >= order


def forward_rows(rows, entry):
    table, order = entry
    n = rows.shape[0]
    d = dot(split_rows(compact(rows)), table[...])
    return jnp.where(degree_mask(n, order), d[:n] + d[n:], 0.0)


def backward_rows(rows, entry):
    table, order = entry
    n = rows.shape[0]
    d = dot_t(split_rows(jnp.where(degree_mask(n, order), rows[:, :L], 0.0)), table[...])
    return expand(jnp.where(order < L, d[:n] + d[n:], 0.0))


def analysis_one(info_ref, x_ref, w_ref, m0, m1, out_ref):
    w = w_ref[...]
    for s, table in slot_tables(0, info_ref, (m0, m1)):
        out_ref[:, s, 0:L] = forward_rows(x_ref[:, s, :] * w, table)
        out_ref[:, s, L:] = jnp.zeros((2, LP - L), F32)


def analysis_fields(first_step, carry, info_ref, x_ref, w_ref, m0, m1, out_ref):
    w = w_ref[...]
    for s, table in slot_tables(first_step, info_ref, (m0, m1)):
        rows = x_ref[:, s, :]
        q0, q1 = halves(rows[:8], rows[8:])
        d = forward_rows(jnp.concatenate([q0 * w, q1 * w], axis=0), table)
        out_ref[0, s, :, 0:L] = d[:8]
        out_ref[1, s, :, 0:L] = d[8:]
        rest = jnp.zeros((8, LP - L), F32)
        out_ref[1, s, :, L:] = rest
        if carry:
            rest = jnp.broadcast_to((rows[:8] + rows[8:])[:, 48:49], (8, LP - L))
        out_ref[0, s, :, L:] = rest


def analysis_sum(info_ref, x_ref, kap_ref, m0, m1, out_ref):
    kap = kap_ref[:, :, :L]
    for s, table in slot_tables(0, info_ref, (m0, m1)):
        parts = []
        for w in range(2):
            rows = x_ref[:, w, s, :]
            parts += list(halves(rows[:8], rows[8:]))
        d = forward_rows(jnp.concatenate(parts, axis=0), table)
        for q in range(2):
            both = d[8 * q : 8 * q + 8] * kap[0] + d[16 + 8 * q : 24 + 8 * q] * kap[1]
            out_ref[q, pl.ds(s, 1), 0:L] = jnp.sum(both, axis=0, keepdims=True)
            out_ref[q, pl.ds(s, 1), L:] = jnp.zeros((1, LP - L), F32)


def in_order(info_ref, mine, other):
    even = info_ref[1] == 0
    return jnp.where(even, mine, other), jnp.where(even, other, mine)


def residual_of(info_ref, mcov_ref, ocov_ref, target_ref):
    lane = L - (LP - 128)
    cov, _ = in_order(info_ref, mcov_ref[0][:, lane : lane + 1], ocov_ref[0][:, lane : lane + 1])
    return cov / (NTHETA * NPHI) - target_ref[...]


def both_halves(d, extra=None):
    h0, h1 = halves(d[:8], d[8:])
    out = jnp.concatenate([h0, h1], axis=0)
    if extra is not None:
        lanes = lax.broadcasted_iota(jnp.int32, out.shape, 1) % 64
        out = jnp.where(lanes >= 48, jnp.concatenate([extra, extra], axis=0), out)
    return out


def synthesis_base(info_ref, mine_ref, other_ref, kap_ref, m0, m1, out_ref):
    kap = kap_ref[...]
    for s, table in slot_tables(0, info_ref, (m0, m1)):
        b0, b1 = in_order(info_ref, mine_ref[pl.ds(s, 1), :], other_ref[pl.ds(s, 1), :])
        rows = jnp.concatenate([kap[0] * b0, kap[0] * b1, kap[1] * b0, kap[1] * b1], axis=0)
        d = backward_rows(rows, table)
        for w in range(2):
            out_ref[:, w, s, :] = both_halves(d[16 * w : 16 * w + 16])


def synthesis_fields(first_step, carry, info_ref, mine_ref, other_ref, kap_ref, w_ref, mcov_ref, ocov_ref, target_ref, m0, m1, *refs):
    out_ref = refs[-1]
    kap = kap_ref[...]
    w = w_ref[...]
    residual = None
    if carry:
        residual = residual_of(info_ref, mcov_ref, ocov_ref, target_ref)
        kap = kap * residual
    for s, table in slot_tables(first_step, info_ref, (m0, m1)):
        b0, b1 = in_order(info_ref, mine_ref[s], other_ref[s])
        d = backward_rows(jnp.concatenate([b0 * kap, b1 * kap], axis=0), table) * w
        out_ref[:, s, :] = both_halves(d, residual)


def synthesis_last(info_ref, mine_ref, other_ref, w_ref, m0, m1, out_ref):
    w = w_ref[...]
    for s, table in slot_tables(0, info_ref, (m0, m1)):
        b0, b1 = in_order(info_ref, mine_ref[pl.ds(s, 1), :], other_ref[pl.ds(s, 1), :])
        out_ref[:, s, :] = backward_rows(jnp.concatenate([b0, b1], axis=0), table) * w


def whole(*shape):
    return pl.BlockSpec(shape, lambda i, *_: (0,) * len(shape))


ROW_SPEC = pl.BlockSpec((SB, LP), lambda i, *_: (i, 0))
PLANE_SPEC = pl.BlockSpec((2, SB, LP), lambda i, *_: (0, i, 0))
COV_SPEC = pl.BlockSpec((1, 8, 128), lambda i, *_: (0, 0, LP // 128 - 1))
PLANE_SHAPE = jax.ShapeDtypeStruct((2, SP, LP), F32)
SENT_PAIR_SHAPE = jax.ShapeDtypeStruct((ORD, 2, SP, 128), F32)
SENT_SHAPE = jax.ShapeDtypeStruct((ORD, SP, 128), F32)


def table_specs(first_step):
    def spec(part):
        return pl.BlockSpec((4, 96, L), lambda i, info: (quad_index(i + first_step, part, info[0]), 0, 0))

    return [spec(0), spec(1)]


def sent_spec(first_step=0):
    return pl.BlockSpec((ORD, SB, 128), lambda i, *_: (0, i + first_step, 0))


def sent_pair_spec():
    return pl.BlockSpec((ORD, 2, SB, 128), lambda i, *_: (0, 0, i, 0))


def cost(flops, nbytes):
    return pl.CostEstimate(flops=int(flops), bytes_accessed=int(nbytes), transcendentals=0)


def leg_call(kernel, steps, first_step, specs, out_spec, out_shape, rows, name, aliases=None, extra=()):
    n = steps * SB
    return pl.pallas_call(
        kernel,
        grid_spec=pltpu.PrefetchScalarGridSpec(
            num_scalar_prefetch=1,
            grid=(steps,),
            in_specs=specs + table_specs(first_step) + list(extra),
            out_specs=out_spec,
        ),
        out_shape=out_shape,
        input_output_aliases=aliases or {},
        compiler_params=params(),
        cost_estimate=cost(2 * n * rows * 128 * LP, n * 96 * LP * 2 + n * rows * LP * 2),
        name=name,
    )


def run_analysis_one(info, x, w, m):
    specs = [pl.BlockSpec((2, SB, 128), lambda i, *_: (0, i, 0)), whole(1, 128)]
    return leg_call(analysis_one, STEPS, 0, specs, PLANE_SPEC, PLANE_SHAPE, 4, "analysis_one")(info, x, w, m, m)


def run_analysis_fields(info, x, w, m, first_step, steps, carry):
    specs = [sent_spec(first_step), whole(1, 128)]
    return leg_call(
        functools.partial(analysis_fields, first_step, carry), steps, first_step, specs,
        pl.BlockSpec((2, SB, 8, LP), lambda i, *_: (0, i, 0, 0)),
        jax.ShapeDtypeStruct((2, steps * SB, 8, LP), F32), 32, "analysis_fields",
    )(info, x, w, m, m)


def run_analysis_sum(info, x, kap, m):
    specs = [sent_pair_spec(), whole(2, 8, LP)]
    return leg_call(analysis_sum, STEPS, 0, specs, PLANE_SPEC, PLANE_SHAPE, 64, "analysis_sum")(info, x, kap, m, m)


def run_synthesis_base(info, mine, other, kap, m):
    specs = [ROW_SPEC, ROW_SPEC, whole(2, 8, LP)]
    return leg_call(
        synthesis_base, STEPS, 0, specs, sent_pair_spec(), SENT_PAIR_SHAPE, 64, "synthesis_base"
    )(info, mine, other, kap, m, m)


def run_synthesis_fields(info, fields, kap, w, m, target, carry):
    out = None
    field = pl.BlockSpec((SB, 8, LP), lambda i, *_: (i, 0, 0))
    specs = [field, field, whole(8, LP), whole(1, 128), COV_SPEC, COV_SPEC, whole(8, 1)]
    mcov, ocov = fields[0]
    for (first_step, steps), (mine, other) in zip(((0, HALF), (HALF, HALF)), fields):
        operands = [info, mine, other, kap, w, mcov, ocov, target, m, m]
        aliases, extra = None, ()
        if out is not None:
            aliases, extra = {len(operands): 0}, (pl.BlockSpec(memory_space=pl.ANY),)
            operands.append(out)
        out = leg_call(
            functools.partial(synthesis_fields, first_step, carry), steps, first_step, specs,
            sent_spec(first_step), SENT_SHAPE, 32, "synthesis_fields", aliases, extra,
        )(*operands)
    return out


def run_synthesis_last(info, mine, other, w, m):
    specs = [ROW_SPEC, ROW_SPEC, whole(1, 128)]
    return leg_call(
        synthesis_last, STEPS, 0, specs, pl.BlockSpec((2, SB, 128), lambda i, *_: (0, i, 0)),
        jax.ShapeDtypeStruct((2, SP, 128), F32), 4, "synthesis_last",
    )(info, mine, other, w, m, m)


def store_split(x, high_ref, low_ref):
    high = x.astype(BF16)
    high_ref[...] = high
    low_ref[...] = (x - high.astype(F32)).astype(BF16)


def product(w_high, w_low, x_high, x_low):
    n = x_high.shape[1]
    if n > 128:
        return dot(w_high, x_high) + dot(w_high, x_low) + dot(w_low, x_high)
    both = dot(w_high, jnp.concatenate([x_high, x_low], axis=1))
    return both[:, :n] + both[:, n:] + dot(w_low, x_high)


def forward_step(values, high_w, low_w):
    high = values.astype(BF16)
    low = (values - high.astype(F32)).astype(BF16)
    return product(high_w, low_w, high, low)


def pack_parts(z, eta):
    low = lane_low(z.shape)
    other = swap(z)
    return jnp.where(low, z, other) * eta, jnp.where(low, other, z) * eta


def mod(maps):
    squares = maps * maps
    return jnp.sqrt(squares + swap(squares) + MOD_EPSILON)


def inverse_step(ic, iss, w_ref):
    even = product(w_ref[0], w_ref[1], ic[0][...], ic[1][...])
    odd = product(w_ref[2], w_ref[3], iss[0][...], iss[1][...])
    return even + odd, even - odd


def accumulate(yc_ref, ys_ref, up, down, t_ref):
    c = forward_step(up + down, t_ref[0], t_ref[1])
    s = forward_step(up - down, t_ref[2], t_ref[3])

    @pl.when(pl.program_id(0) == 0)
    def _():
        yc_ref[...] = c
        ys_ref[...] = s

    @pl.when(pl.program_id(0) > 0)
    def _():
        yc_ref[...] += c
        ys_ref[...] += s


def sum_parts(yc, ys, eta):
    vc, vs = yc * eta, ys * eta
    return jnp.where(lane_low(vc.shape), vc + swap(vc), vs + swap(vs))


def is_last():
    return pl.program_id(0) == pl.num_programs(0) - 1


def start_inverse(z_ref, eta, ch, cl, sh, sl):
    @pl.when(pl.program_id(0) == 0)
    def _():
        c, s = pack_parts(z_ref[...].reshape(SA, 128), eta)
        store_split(c, ch, cl)
        store_split(s, sh, sl)


def longitude_first(
    z_ref, eta_ref, w_ref, t_ref, out_ref, first_ref, pair_ref, ch, cl, sh, sl, yc, ys,
):
    @pl.when(pl.program_id(0) == 0)
    def _():
        eta = eta_ref[...]
        parts = [pack_parts(z_ref[:, w].reshape(SA, 128), eta) for w in range(2)]
        store_split(jnp.concatenate([parts[0][0], parts[1][0]], axis=1), ch, cl)
        store_split(jnp.concatenate([parts[0][1], parts[1][1]], axis=1), sh, sl)

    maps = inverse_step((ch, cl), (sh, sl), w_ref)
    for i in range(2):
        first_ref[i] = maps[i][:, :128]
        pair_ref[i] = maps[i][:, 128:]
    accumulate(yc, ys, mod(maps[0][:, :128]), mod(maps[1][:, :128]), t_ref)

    @pl.when(is_last())
    def _():
        out_ref[...] = jnp.where(lane_low((SA, 128)), yc[...], ys[...]).reshape(ORD, SP, 128)


def longitude_second(
    z_ref, eta_ref, weight_ref, pair_ref, w_ref, t_ref,
    out_ref, ratio_ref, ch, cl, sh, sl, yc, ys, cov,
):
    start_inverse(z_ref, eta_ref[...], ch, cl, sh, sl)

    @pl.when(pl.program_id(0) == 0)
    def _():
        cov[...] = jnp.zeros_like(cov)

    maps = inverse_step((ch, cl), (sh, sl), w_ref)
    weight = weight_ref[...]
    k = lax.broadcasted_iota(jnp.int32, (KT, 128), 0) + KT * pl.program_id(0)
    grads = []
    total = 0.0
    for i in range(2):
        second_mod = mod(maps[i])
        pair_mod = mod(pair_ref[i])
        total += pair_mod * second_mod
        grads.append(maps[i] * (weight * pair_mod / second_mod))
        ratio_ref[i] = pair_ref[i] * (weight * second_mod / pair_mod)
    cov[...] += jnp.sum(total * fold_weights(k), axis=0, keepdims=True) * weight
    accumulate(yc, ys, grads[0], grads[1], t_ref)

    @pl.when(is_last())
    def _():
        lanes = lax.broadcasted_iota(jnp.int32, (1, 128), 1)
        value = jnp.sum(jnp.where(lanes < 48, cov[...], 0.0), axis=1, keepdims=True)
        out = sum_parts(yc[...], ys[...], eta_ref[...])
        lanes = lax.broadcasted_iota(jnp.int32, (SA, 128), 1) % 64
        out_ref[...] = jnp.where(lanes >= 48, value, out).reshape(ORD, SP, 128)


def longitude_third(
    z_ref, eta_ref, first_ref, ratio_ref, w_ref, t_ref, out_ref, ch, cl, sh, sl, yc, ys,
):
    start_inverse(z_ref, 1.0, ch, cl, sh, sl)
    maps = inverse_step((ch, cl), (sh, sl), w_ref)
    residual = z_ref[0, 0:1, 48:49]
    grads = []
    for i in range(2):
        first = first_ref[i]
        grads.append(jnp.concatenate([first * (maps[i] / mod(first)), ratio_ref[i] * residual], axis=1))
    accumulate(yc, ys, grads[0], grads[1], t_ref)

    @pl.when(is_last())
    def _():
        eta = eta_ref[...]
        for w in range(2):
            part = slice(128 * w, 128 * w + 128)
            out_ref[:, w] = sum_parts(yc[:, part], ys[:, part], eta).reshape(ORD, SP, 128)


W_SPEC = pl.BlockSpec((4, KT, SA), lambda i: (0, i, 0))
T_SPEC = pl.BlockSpec((4, SA, KT), lambda i: (0, 0, i))
MAP_SPEC = pl.BlockSpec((2, KT, 128), lambda i: (0, i, 0))
MAP_SHAPE = jax.ShapeDtypeStruct((2, KP, 128), F32)


def lon_scratch(n_in, n_out):
    return [pltpu.VMEM((SA, n_in), BF16)] * 4 + [pltpu.VMEM((SA, n_out), F32)] * 2


def lon_call(kernel, specs, outs, scratch, name):
    n = len(scratch) // 2
    return pl.pallas_call(
        kernel,
        grid=(KP // KT,),
        in_specs=specs,
        out_specs=[o[0] for o in outs],
        out_shape=[o[1] for o in outs],
        scratch_shapes=scratch,
        compiler_params=params(LON_VMEM),
        cost_estimate=cost(6 * n * KP * SA * 128, 4 * KP * SA * 2 + 3 * KP * 128 * 4),
        name=name,
    )


SENT_PAIR = (whole(ORD, 2, SP, 128), SENT_PAIR_SHAPE)
SENT = (whole(ORD, SP, 128), SENT_SHAPE)
MAPS = (MAP_SPEC, MAP_SHAPE)
LANES = whole(SA, 128)


def run_longitude_first(z, eta, waves):
    specs = [SENT_PAIR[0], LANES] + [W_SPEC, T_SPEC]
    return lon_call(longitude_first, specs, [SENT, MAPS, MAPS], lon_scratch(256, 128), "longitude_first")(
        z, eta, *waves
    )


def run_longitude_second(z, eta, weight, pair, waves):
    specs = [SENT[0], LANES, whole(1, 128), MAP_SPEC] + [W_SPEC, T_SPEC]
    scratch = lon_scratch(128, 128) + [pltpu.VMEM((1, 128), F32)]
    return lon_call(longitude_second, specs, [SENT, MAPS], scratch, "longitude_second")(
        z, eta, weight, pair, *waves
    )


def run_longitude_third(z, eta, first, ratio, waves):
    specs = [SENT[0], LANES, MAP_SPEC, MAP_SPEC] + [W_SPEC, T_SPEC]
    return lon_call(longitude_third, specs, [SENT_PAIR], lon_scratch(128, 256), "longitude_third")(
        z, eta, first, ratio, *waves
    )[0]


def angle(product_of):
    return (product_of % NPHI).astype(F32) * (2.0 * math.pi / NPHI)


def wave_tables(slots, valid):
    scale = jnp.where(valid, NORMING, 0.0).astype(F32)
    tables = []
    for step, count in ((32, KP // 32), (1, 32)):
        phase = angle(jnp.arange(count, dtype=jnp.int32)[:, None] * step * slots[None, :])
        tables.append(jnp.stack([jnp.cos(phase), jnp.sin(phase)]) * (scale[None, None, :] if step > 1 else 1.0))
    for step in (128, 1):
        phase = angle(jnp.arange(128, dtype=jnp.int32)[None, :] * step * slots[:, None])
        tables.append(jnp.stack([jnp.cos(phase), jnp.sin(phase)]) * (scale[None, :, None] if step > 1 else 1.0))
    return tables


def fill_waves(coarse_ref, fine_ref, tcoarse_ref, tfine_ref, w_ref, t_ref):
    i = pl.program_id(0)
    cb, sb = fine_ref[0], fine_ref[1]
    for j in range(4):
        ca, sa = [coarse_ref[part, pl.ds(4 * i + j, 1), :] for part in range(2)]
        k = lax.broadcasted_iota(jnp.int32, (32, SA), 0) + (128 * i + 32 * j)
        keep = k <= NPHI // 2
        rows = pl.ds(32 * j, 32)
        for value, high, low in ((ca * cb - sa * sb, 0, 1), (sa * cb + ca * sb, 2, 3)):
            value = jnp.where(keep, value, 0.0)
            head = value.astype(BF16)
            w_ref[high, rows, :] = head
            w_ref[low, rows, :] = (value - head.astype(F32)).astype(BF16)
    cb, sb = tfine_ref[0], tfine_ref[1]
    for j in range(KP // 128):
        ca, sa = tcoarse_ref[0][:, j : j + 1], tcoarse_ref[1][:, j : j + 1]
        k = lax.broadcasted_iota(jnp.int32, (1, 128), 1) + 128 * j
        fold = fold_weights(k)
        cols = pl.ds(128 * j, 128)
        for value, high, low in ((ca * cb - sa * sb, 0, 1), (sa * cb + ca * sb, 2, 3)):
            value = value * fold
            head = value.astype(BF16)
            t_ref[high, :, cols] = head
            t_ref[low, :, cols] = (value - head.astype(F32)).astype(BF16)


def make_waves(tables):
    slot_rows = pl.BlockSpec((2, 128, 128), lambda i: (0, i, 0))
    return pl.pallas_call(
        fill_waves,
        grid=(KP // 128,),
        in_specs=[whole(2, KP // 32, SA), whole(2, 32, SA), slot_rows, slot_rows],
        out_specs=[pl.BlockSpec((4, 128, SA), lambda i: (0, i, 0))] * 2,
        out_shape=[pltpu.HBM((4, KP, SA), BF16)] * 2,
        compiler_params=params(),
        cost_estimate=cost(32 * KP * SA, 16 * KP * SA),
        name="fill_waves",
    )(*tables)


def fold_weights(k):
    return jnp.where((k == 0) | (k == NPHI // 2), 0.5, jnp.where(k < NPHI // 2, 1.0, 0.0))


def pad_cycles(x):
    lead = x.shape[:-1]
    x = x.reshape(lead + (2, 48))
    return jnp.pad(x, [(0, 0)] * len(lead) + [(0, 0), (0, 16)]).reshape(lead + (128,))


def pad_degrees(x):
    return jnp.pad(x, [(0, 0)] * (x.ndim - 1) + [(0, LP - L)])


def ord_exchange(x):
    return lax.all_to_all(x, "ord", split_axis=0, concat_axis=0, tiled=True)


def ord_gather(x):
    return ord_exchange(jnp.broadcast_to(x[None], (ORD,) + x.shape))


def core_swap(x):
    return lax.ppermute(x, "lat", [(i, i ^ 1) for i in range(LAT)])


def z_shift(x, step):
    return lax.ppermute(x, "lat", [(i, (i + 2 * step) % LAT) for i in range(LAT)])


def core_sum(parts, core):
    mine = lax.dynamic_index_in_dim(parts, core, 0, keepdims=False)
    away = lax.dynamic_index_in_dim(parts, 1 - core, 0, keepdims=False)
    return mine + core_swap(away)


def turn_blocks(x, count):
    return jnp.concatenate([x[count * ZB :], x[: count * ZB]], axis=0)


def lat_sum_small(parts, core):
    mine = core_sum(parts, core)
    there = [z_shift(mine, step) for step in range(1, 4)]
    total = mine
    for step in range(1, 4):
        total = total + turn_blocks(there[step - 1], step)
    return total, core_swap(total)


def lat_sum_large(high, low, core):
    high = core_sum(high, core)
    there = z_shift(high[:ZB], 2), z_shift(high[ZB:], 3)
    low = core_sum(low, core)
    own = low[:ZB] + there[0] + z_shift(low[ZB:], 1) + there[1]
    blocks = [own, z_shift(own, 3), z_shift(own, 2), z_shift(own, 1)]
    others = [core_swap(x) for x in blocks]
    return [
        (jnp.concatenate(blocks[i : i + 2], axis=0), jnp.concatenate(others[i : i + 2], axis=0)) for i in (0, 2)
    ]


def after(x, *done):
    return lax.optimization_barrier((x,) + done)[0]


def shards(grid_field, legendre, cycle_weight, slot_order, kappa, eta, pairs, target):
    me = lax.axis_index("ord")
    z, core = lax.axis_index("lat") // 2, lax.axis_index("lat") % 2
    info = jnp.stack([z, core]).astype(jnp.int32)
    direction = me % 4

    field = jnp.pad(pad_cycles(grid_field), [(0, 6), (0, 0)])
    field_all = ord_gather(field).reshape(ORD * 96, 128)

    position = jnp.arange(SP, dtype=jnp.int32)
    quad = quad_index(position // SB, position // 4 % 2, z)
    place = quad * 4 + position % 4
    slots2 = jnp.pad(slot_order.reshape(ORD, SLOT), [(0, 0), (0, SP - SLOT)])
    slots2 = jnp.sum(jnp.where(place[None, :, None] == position[None, None, :], slots2[:, None, :], 0), axis=2)
    own_valid = place < SLOT
    slots = slots2.reshape(SA)
    valid = jnp.broadcast_to(own_valid, (ORD, SP)).reshape(SA)
    my_slots = lax.dynamic_index_in_dim(slots2, me, 0, keepdims=False)
    degree_ids = jnp.arange(L, dtype=jnp.int32)
    info = jnp.concatenate([info, jnp.where(own_valid, my_slots, L)])
    table = jnp.transpose(legendre, (1, 0, 2))

    offset = jnp.arange(96, dtype=jnp.int32)
    longitude = (jnp.arange(ORD, dtype=jnp.int32)[:, None] * 90 + offset[None, :]).reshape(ORD * 96)
    k_valid = jnp.broadcast_to(offset < 90, (ORD, 96)).reshape(ORD * 96)
    phase = angle(my_slots[:, None] * longitude[None, :])
    own_scale = jnp.where(own_valid[:, None] & k_valid[None, :], NORMING, 0.0).astype(F32)
    own_waves = jnp.stack([jnp.cos(phase) * own_scale, jnp.sin(phase) * own_scale]).reshape(2 * SP, ORD * 96)

    weight_lanes = pad_cycles(cycle_weight[None, :])
    own_waves, *tables = lax.optimization_barrier((own_waves, *wave_tables(slots, valid)))
    spectra = jnp.dot(own_waves, field_all, precision=HIGHEST_PREC).reshape(2, SP, 128)
    parts = run_analysis_one(info, spectra, weight_lanes, table)

    eta_rows = lax.dynamic_index_in_dim(eta, direction, 0, keepdims=False)
    hit = slots[:, None] == degree_ids[None, :]
    eta_cols = [jnp.sum(jnp.where(hit, eta_rows[r][None, :], 0.0), axis=1, keepdims=True) for r in range(2)]
    eta_lanes = jnp.where(jnp.arange(128)[None, :] < 64, eta_cols[0], eta_cols[1])

    scale_ids = jnp.arange(kappa.shape[0], dtype=jnp.int32)
    picks = [(pairs[:, i : i + 1] == scale_ids[None, :]).astype(F32) for i in range(2)]
    kaps = [pad_degrees(jnp.sum(pick[:, :, None] * kappa[None], axis=1)) for pick in picks]
    kap_rows = jnp.stack([jnp.repeat(kap, 4, axis=0) for kap in kaps])
    kap_second = kap_rows[1]
    target_rows = target.reshape(8, 1)
    ones = jnp.ones((1, 128), F32)
    my_weight = lax.dynamic_index_in_dim(weight_lanes.reshape(2, 64), me // 8, 0, keepdims=True)
    my_weight = jnp.concatenate([my_weight, my_weight], axis=1)

    def all_sums(x, w, carry):
        high = run_analysis_fields(info, x, w, table, HALF, HALF, carry)
        low = run_analysis_fields(info, x, after(w, high), table, 0, HALF, carry)
        return lat_sum_large(high, low, core)

    mine, other = lat_sum_small(parts, core)
    cycles = run_synthesis_base(info, mine, other, kap_rows, table)
    z_first = ord_exchange(cycles)
    waves = make_waves(after(tables, cycles))
    spectra, first_maps, pair_maps = run_longitude_first(z_first, eta_lanes, waves)
    sums = all_sums(ord_exchange(spectra), weight_lanes, False)
    z_second = ord_exchange(run_synthesis_fields(info, sums, kap_second, ones, table, target_rows, False))
    spectra, ratio = run_longitude_second(z_second, eta_lanes, my_weight, pair_maps, waves)
    sums = all_sums(ord_exchange(spectra), ones, True)
    z_third = ord_exchange(run_synthesis_fields(info, sums, kap_second, weight_lanes, table, target_rows, True))
    spectra = run_longitude_third(z_third, eta_lanes, first_maps, ratio, waves)
    mine, other = lat_sum_small(run_analysis_sum(info, ord_exchange(spectra), kap_rows, table), core)
    cycles = run_synthesis_last(info, mine, other, weight_lanes, table)

    end_slots = after(slots, z_third)
    phase = angle((me * 90 + offset)[:, None] * end_slots[None, :])
    end_scale = jnp.where(valid[None, :], NORMING, 0.0).astype(F32)
    end_waves = jnp.stack(
        [(jnp.cos(phase) * end_scale).reshape(96, ORD, SP), (jnp.sin(phase) * end_scale).reshape(96, ORD, SP)], axis=2
    ).reshape(96, ORD * 2 * SP)
    cycles_all = ord_gather(cycles.reshape(2 * SP, 128)).reshape(ORD * 2 * SP, 128)
    result = jnp.dot(end_waves, cycles_all, precision=HIGHEST_PREC)
    return result[:90].reshape(90, 2, 64)[:, :, :48].reshape(90, 96)


def solution(mesh):
    return jax.shard_map(
        shards,
        mesh=mesh,
        in_specs=(P("ord", "lat"), P("lat", "ord", None), P("lat"), P(), P(), P(), P(), P()),
        out_specs=P("ord", "lat"),
        check_vma=False,
    )
```

```python
import functools
import math

import jax
import jax.numpy as jnp
from jax import lax
from jax.experimental import pallas as pl
from jax.experimental.pallas import tpu as pltpu
from jax.sharding import PartitionSpec as P

F32 = jnp.float32
BF16 = jnp.bfloat16
HIGHEST_PREC = lax.Precision.HIGHEST
MOD_EPSILON = 0.01
L = 720
NPHI = 1440
NTHETA = 768
LAT = 8
ORD = 16
SLOT = 45
SP = 48
SA = ORD * SP
LP = 768
KP = 768
SB = 8
STEPS = SP // SB
HALF = STEPS // 2
ZB = SP // 4
KT = 256
NORMING = math.sqrt(2.0 / NPHI)
VMEM = 16 * 1024 * 1024
LON_VMEM = 54 * 1024 * 1024


def params(limit=VMEM):
    return pltpu.CompilerParams(vmem_limit_bytes=limit)


def lane_low(shape):
    return lax.broadcasted_iota(jnp.int32, shape, len(shape) - 1) % 128 < 64


def swap(x):
    return pltpu.roll(x, 64, x.ndim - 1)


def halves(first, second):
    low = lane_low(first.shape)
    return jnp.where(low, first, swap(second)), jnp.where(low, swap(first), second)


def split_rows(x):
    high = x.astype(BF16).astype(F32)
    return jnp.concatenate([high, x - high], axis=0).astype(BF16)


def dot(a, b):
    return lax.dot_general(a, b, (((1,), (0,)), ((), ())), preferred_element_type=F32)


def dot_t(a, b):
    return lax.dot_general(a, b, (((1,), (1,)), ((), ())), preferred_element_type=F32)


def compact(x):
    low = lax.broadcasted_iota(jnp.int32, x.shape, 1) < 48
    return jnp.where(low, x, pltpu.roll(x, 112, 1))[:, :96]


def expand(y):
    y = jnp.concatenate([y, jnp.zeros((y.shape[0], 32), F32)], axis=1)
    low = lax.broadcasted_iota(jnp.int32, y.shape, 1) < 48
    return jnp.where(low, y, pltpu.roll(y, 16, 1))


def quad_index(step, part, z):
    quad = 2 * step + part
    return lax.rem(z + lax.div(quad, 3), 4) * 3 + lax.rem(quad, 3)


def slot_tables(first_step, info_ref, tables):
    step = pl.program_id(0) + first_step
    for s in range(SB):
        yield s, (tables[s // 4].at[s % 4], info_ref[2 + step * SB + s])


def degree_mask(rows, order):
    return lax.broadcasted_iota(jnp.int32, (rows, L), 1) >= order


def forward_rows(rows, entry):
    table, order = entry
    n = rows.shape[0]
    d = dot(split_rows(compact(rows)), table[...])
    return jnp.where(degree_mask(n, order), d[:n] + d[n:], 0.0)


def backward_rows(rows, entry):
    table, order = entry
    n = rows.shape[0]
    d = dot_t(split_rows(jnp.where(degree_mask(n, order), rows[:, :L], 0.0)), table[...])
    return expand(jnp.where(order < L, d[:n] + d[n:], 0.0))


def analysis_one(info_ref, x_ref, w_ref, m0, m1, out_ref):
    w = w_ref[...]
    for s, table in slot_tables(0, info_ref, (m0, m1)):
        out_ref[:, s, 0:L] = forward_rows(x_ref[:, s, :] * w, table)
        out_ref[:, s, L:] = jnp.zeros((2, LP - L), F32)


def analysis_fields(first_step, carry, info_ref, x_ref, w_ref, m0, m1, out_ref):
    w = w_ref[...]
    for s, table in slot_tables(first_step, info_ref, (m0, m1)):
        rows = x_ref[:, s, :]
        q0, q1 = halves(rows[:8], rows[8:])
        d = forward_rows(jnp.concatenate([q0 * w, q1 * w], axis=0), table)
        out_ref[0, s, :, 0:L] = d[:8]
        out_ref[1, s, :, 0:L] = d[8:]
        rest = jnp.zeros((8, LP - L), F32)
        out_ref[1, s, :, L:] = rest
        if carry:
            rest = jnp.broadcast_to((rows[:8] + rows[8:])[:, 48:49], (8, LP - L))
        out_ref[0, s, :, L:] = rest


def analysis_sum(info_ref, x_ref, kap_ref, m0, m1, out_ref):
    kap = kap_ref[:, :, :L]
    for s, table in slot_tables(0, info_ref, (m0, m1)):
        parts = []
        for w in range(2):
            rows = x_ref[:, w, s, :]
            parts += list(halves(rows[:8], rows[8:]))
        d = forward_rows(jnp.concatenate(parts, axis=0), table)
        for q in range(2):
            both = d[8 * q : 8 * q + 8] * kap[0] + d[16 + 8 * q : 24 + 8 * q] * kap[1]
            out_ref[q, pl.ds(s, 1), 0:L] = jnp.sum(both, axis=0, keepdims=True)
            out_ref[q, pl.ds(s, 1), L:] = jnp.zeros((1, LP - L), F32)


def in_order(info_ref, mine, other):
    even = info_ref[1] == 0
    return jnp.where(even, mine, other), jnp.where(even, other, mine)


def residual_of(info_ref, mcov_ref, ocov_ref, target_ref):
    lane = L - (LP - 128)
    cov, _ = in_order(info_ref, mcov_ref[0][:, lane : lane + 1], ocov_ref[0][:, lane : lane + 1])
    return cov / (NTHETA * NPHI) - target_ref[...]


def both_halves(d, extra=None):
    h0, h1 = halves(d[:8], d[8:])
    out = jnp.concatenate([h0, h1], axis=0)
    if extra is not None:
        lanes = lax.broadcasted_iota(jnp.int32, out.shape, 1) % 64
        out = jnp.where(lanes >= 48, jnp.concatenate([extra, extra], axis=0), out)
    return out


def synthesis_base(info_ref, mine_ref, other_ref, kap_ref, m0, m1, out_ref):
    kap = kap_ref[...]
    for s, table in slot_tables(0, info_ref, (m0, m1)):
        b0, b1 = in_order(info_ref, mine_ref[pl.ds(s, 1), :], other_ref[pl.ds(s, 1), :])
        rows = jnp.concatenate([kap[0] * b0, kap[0] * b1, kap[1] * b0, kap[1] * b1], axis=0)
        d = backward_rows(rows, table)
        for w in range(2):
            out_ref[:, w, s, :] = both_halves(d[16 * w : 16 * w + 16])


def synthesis_fields(first_step, carry, info_ref, mine_ref, other_ref, kap_ref, w_ref, mcov_ref, ocov_ref, target_ref, m0, m1, *refs):
    out_ref = refs[-1]
    kap = kap_ref[...]
    w = w_ref[...]
    residual = None
    if carry:
        residual = residual_of(info_ref, mcov_ref, ocov_ref, target_ref)
        kap = kap * residual
    for s, table in slot_tables(first_step, info_ref, (m0, m1)):
        b0, b1 = in_order(info_ref, mine_ref[s], other_ref[s])
        d = backward_rows(jnp.concatenate([b0 * kap, b1 * kap], axis=0), table) * w
        out_ref[:, s, :] = both_halves(d, residual)


def synthesis_last(info_ref, mine_ref, other_ref, w_ref, m0, m1, out_ref):
    w = w_ref[...]
    for s, table in slot_tables(0, info_ref, (m0, m1)):
        b0, b1 = in_order(info_ref, mine_ref[pl.ds(s, 1), :], other_ref[pl.ds(s, 1), :])
        out_ref[:, s, :] = backward_rows(jnp.concatenate([b0, b1], axis=0), table) * w


def whole(*shape):
    return pl.BlockSpec(shape, lambda i, *_: (0,) * len(shape))


ROW_SPEC = pl.BlockSpec((SB, LP), lambda i, *_: (i, 0))
PLANE_SPEC = pl.BlockSpec((2, SB, LP), lambda i, *_: (0, i, 0))
COV_SPEC = pl.BlockSpec((1, 8, 128), lambda i, *_: (0, 0, LP // 128 - 1))
PLANE_SHAPE = jax.ShapeDtypeStruct((2, SP, LP), F32)
SENT_PAIR_SHAPE = jax.ShapeDtypeStruct((ORD, 2, SP, 128), F32)
SENT_SHAPE = jax.ShapeDtypeStruct((ORD, SP, 128), F32)


def table_specs(first_step):
    def spec(part):
        return pl.BlockSpec((4, 96, L), lambda i, info: (quad_index(i + first_step, part, info[0]), 0, 0))

    return [spec(0), spec(1)]


def sent_spec(first_step=0):
    return pl.BlockSpec((ORD, SB, 128), lambda i, *_: (0, i + first_step, 0))


def sent_pair_spec():
    return pl.BlockSpec((ORD, 2, SB, 128), lambda i, *_: (0, 0, i, 0))


def cost(flops, nbytes):
    return pl.CostEstimate(flops=int(flops), bytes_accessed=int(nbytes), transcendentals=0)


def leg_call(kernel, steps, first_step, specs, out_spec, out_shape, rows, name, aliases=None, extra=()):
    n = steps * SB
    return pl.pallas_call(
        kernel,
        grid_spec=pltpu.PrefetchScalarGridSpec(
            num_scalar_prefetch=1,
            grid=(steps,),
            in_specs=specs + table_specs(first_step) + list(extra),
            out_specs=out_spec,
        ),
        out_shape=out_shape,
        input_output_aliases=aliases or {},
        compiler_params=params(),
        cost_estimate=cost(2 * n * rows * 128 * LP, n * 96 * LP * 2 + n * rows * LP * 2),
        name=name,
    )


def run_analysis_one(info, x, w, m):
    specs = [pl.BlockSpec((2, SB, 128), lambda i, *_: (0, i, 0)), whole(1, 128)]
    return leg_call(analysis_one, STEPS, 0, specs, PLANE_SPEC, PLANE_SHAPE, 4, "analysis_one")(info, x, w, m, m)


def run_analysis_fields(info, x, w, m, first_step, steps, carry):
    specs = [sent_spec(first_step), whole(1, 128)]
    return leg_call(
        functools.partial(analysis_fields, first_step, carry), steps, first_step, specs,
        pl.BlockSpec((2, SB, 8, LP), lambda i, *_: (0, i, 0, 0)),
        jax.ShapeDtypeStruct((2, steps * SB, 8, LP), F32), 32, "analysis_fields",
    )(info, x, w, m, m)


def run_analysis_sum(info, x, kap, m):
    specs = [sent_pair_spec(), whole(2, 8, LP)]
    return leg_call(analysis_sum, STEPS, 0, specs, PLANE_SPEC, PLANE_SHAPE, 64, "analysis_sum")(info, x, kap, m, m)


def run_synthesis_base(info, mine, other, kap, m):
    specs = [ROW_SPEC, ROW_SPEC, whole(2, 8, LP)]
    return leg_call(
        synthesis_base, STEPS, 0, specs, sent_pair_spec(), SENT_PAIR_SHAPE, 64, "synthesis_base"
    )(info, mine, other, kap, m, m)


def run_synthesis_fields(info, fields, kap, w, m, target, carry):
    out = None
    field = pl.BlockSpec((SB, 8, LP), lambda i, *_: (i, 0, 0))
    specs = [field, field, whole(8, LP), whole(1, 128), COV_SPEC, COV_SPEC, whole(8, 1)]
    mcov, ocov = fields[0]
    for (first_step, steps), (mine, other) in zip(((0, STEPS),), fields):
        operands = [info, mine, other, kap, w, mcov, ocov, target, m, m]
        aliases, extra = None, ()
        if out is not None:
            aliases, extra = {len(operands): 0}, (pl.BlockSpec(memory_space=pl.ANY),)
            operands.append(out)
        out = leg_call(
            functools.partial(synthesis_fields, first_step, carry), steps, first_step, specs,
            sent_spec(first_step), SENT_SHAPE, 32, "synthesis_fields", aliases, extra,
        )(*operands)
    return out


def run_synthesis_last(info, mine, other, w, m):
    specs = [ROW_SPEC, ROW_SPEC, whole(1, 128)]
    return leg_call(
        synthesis_last, STEPS, 0, specs, pl.BlockSpec((2, SB, 128), lambda i, *_: (0, i, 0)),
        jax.ShapeDtypeStruct((2, SP, 128), F32), 4, "synthesis_last",
    )(info, mine, other, w, m, m)


def store_split(x, high_ref, low_ref):
    high = x.astype(BF16)
    high_ref[...] = high
    low_ref[...] = (x - high.astype(F32)).astype(BF16)


def product(w_high, w_low, x_high, x_low):
    n = x_high.shape[1]
    if n > 128:
        return dot(w_high, x_high) + dot(w_high, x_low) + dot(w_low, x_high)
    both = dot(w_high, jnp.concatenate([x_high, x_low], axis=1))
    return both[:, :n] + both[:, n:] + dot(w_low, x_high)


def forward_step(values, high_w, low_w):
    high = values.astype(BF16)
    low = (values - high.astype(F32)).astype(BF16)
    return product(high_w, low_w, high, low)


def pack_parts(z, eta):
    low = lane_low(z.shape)
    other = swap(z)
    return jnp.where(low, z, other) * eta, jnp.where(low, other, z) * eta


def mod(maps):
    squares = maps * maps
    return jnp.sqrt(squares + swap(squares) + MOD_EPSILON)


def inverse_step(ic, iss, w_ref):
    even = product(w_ref[0], w_ref[1], ic[0][...], ic[1][...])
    odd = product(w_ref[2], w_ref[3], iss[0][...], iss[1][...])
    return even + odd, even - odd


def accumulate(yc_ref, ys_ref, up, down, t_ref):
    c = forward_step(up + down, t_ref[0], t_ref[1])
    s = forward_step(up - down, t_ref[2], t_ref[3])

    @pl.when(pl.program_id(0) == 0)
    def _():
        yc_ref[...] = c
        ys_ref[...] = s

    @pl.when(pl.program_id(0) > 0)
    def _():
        yc_ref[...] += c
        ys_ref[...] += s


def sum_parts(yc, ys, eta):
    vc, vs = yc * eta, ys * eta
    return jnp.where(lane_low(vc.shape), vc + swap(vc), vs + swap(vs))


def is_last():
    return pl.program_id(0) == pl.num_programs(0) - 1


def start_inverse(z_ref, eta, ch, cl, sh, sl):
    @pl.when(pl.program_id(0) == 0)
    def _():
        c, s = pack_parts(z_ref[...].reshape(SA, 128), eta)
        store_split(c, ch, cl)
        store_split(s, sh, sl)


def longitude_first(
    z_ref, eta_ref, w_ref, t_ref, out_ref, first_ref, pair_ref, ch, cl, sh, sl, yc, ys,
):
    @pl.when(pl.program_id(0) == 0)
    def _():
        eta = eta_ref[...]
        parts = [pack_parts(z_ref[:, w].reshape(SA, 128), eta) for w in range(2)]
        store_split(jnp.concatenate([parts[0][0], parts[1][0]], axis=1), ch, cl)
        store_split(jnp.concatenate([parts[0][1], parts[1][1]], axis=1), sh, sl)

    maps = inverse_step((ch, cl), (sh, sl), w_ref)
    for i in range(2):
        first_ref[i] = maps[i][:, :128]
        pair_ref[i] = maps[i][:, 128:]
    accumulate(yc, ys, mod(maps[0][:, :128]), mod(maps[1][:, :128]), t_ref)

    @pl.when(is_last())
    def _():
        out_ref[...] = jnp.where(lane_low((SA, 128)), yc[...], ys[...]).reshape(ORD, SP, 128)


def longitude_second(
    z_ref, eta_ref, weight_ref, fold_ref, pair_ref, w_ref, t_ref,
    out_ref, ratio_ref, ch, cl, sh, sl, yc, ys, cov,
):
    start_inverse(z_ref, eta_ref[...], ch, cl, sh, sl)

    @pl.when(pl.program_id(0) == 0)
    def _():
        cov[...] = jnp.zeros_like(cov)

    maps = inverse_step((ch, cl), (sh, sl), w_ref)
    weight = weight_ref[...]
    grads = []
    total = 0.0
    for i in range(2):
        second_mod = mod(maps[i])
        pair_mod = mod(pair_ref[i])
        total += pair_mod * second_mod
        grads.append(maps[i] * (weight * pair_mod / second_mod))
        ratio_ref[i] = pair_ref[i] * (weight * second_mod / pair_mod)
    cov[...] += jnp.sum(total * fold_ref[...], axis=0, keepdims=True) * weight
    accumulate(yc, ys, grads[0], grads[1], t_ref)

    @pl.when(is_last())
    def _():
        lanes = lax.broadcasted_iota(jnp.int32, (1, 128), 1)
        value = jnp.sum(jnp.where(lanes < 48, cov[...], 0.0), axis=1, keepdims=True)
        out = sum_parts(yc[...], ys[...], eta_ref[...])
        lanes = lax.broadcasted_iota(jnp.int32, (SA, 128), 1) % 64
        out_ref[...] = jnp.where(lanes >= 48, value, out).reshape(ORD, SP, 128)


def longitude_third(
    z_ref, eta_ref, first_ref, ratio_ref, w_ref, t_ref, out_ref, ch, cl, sh, sl, yc, ys,
):
    start_inverse(z_ref, 1.0, ch, cl, sh, sl)
    maps = inverse_step((ch, cl), (sh, sl), w_ref)
    residual = z_ref[0, 0:1, 48:49]
    grads = []
    for i in range(2):
        first = first_ref[i]
        grads.append(jnp.concatenate([first * (maps[i] / mod(first)), ratio_ref[i] * residual], axis=1))
    accumulate(yc, ys, grads[0], grads[1], t_ref)

    @pl.when(is_last())
    def _():
        eta = eta_ref[...]
        for w in range(2):
            part = slice(128 * w, 128 * w + 128)
            out_ref[:, w] = sum_parts(yc[:, part], ys[:, part], eta).reshape(ORD, SP, 128)


W_SPEC = pl.BlockSpec((4, KT, SA), lambda i: (0, i, 0))
T_SPEC = pl.BlockSpec((4, SA, KT), lambda i: (0, 0, i))
MAP_SPEC = pl.BlockSpec((2, KT, 128), lambda i: (0, i, 0))
MAP_SHAPE = jax.ShapeDtypeStruct((2, KP, 128), F32)


def lon_scratch(n_in, n_out):
    return [pltpu.VMEM((SA, n_in), BF16)] * 4 + [pltpu.VMEM((SA, n_out), F32)] * 2


def lon_call(kernel, specs, outs, scratch, name):
    n = len(scratch) // 2
    return pl.pallas_call(
        kernel,
        grid=(KP // KT,),
        in_specs=specs,
        out_specs=[o[0] for o in outs],
        out_shape=[o[1] for o in outs],
        scratch_shapes=scratch,
        compiler_params=params(LON_VMEM),
        cost_estimate=cost(6 * n * KP * SA * 128, 4 * KP * SA * 2 + 3 * KP * 128 * 4),
        name=name,
    )


SENT_PAIR = (whole(ORD, 2, SP, 128), SENT_PAIR_SHAPE)
SENT = (whole(ORD, SP, 128), SENT_SHAPE)
MAPS = (MAP_SPEC, MAP_SHAPE)
LANES = whole(SA, 128)


def run_longitude_first(z, eta, waves):
    specs = [SENT_PAIR[0], LANES] + [W_SPEC, T_SPEC]
    return lon_call(longitude_first, specs, [SENT, MAPS, MAPS], lon_scratch(256, 128), "longitude_first")(
        z, eta, *waves
    )


def run_longitude_second(z, eta, weight, fold, pair, waves):
    fold_spec = pl.BlockSpec((KT, 128), lambda i: (i, 0))
    specs = [SENT[0], LANES, whole(1, 128), fold_spec, MAP_SPEC] + [W_SPEC, T_SPEC]
    scratch = lon_scratch(128, 128) + [pltpu.VMEM((1, 128), F32)]
    return lon_call(longitude_second, specs, [SENT, MAPS], scratch, "longitude_second")(
        z, eta, weight, fold, pair, *waves
    )


def run_longitude_third(z, eta, first, ratio, waves):
    specs = [SENT[0], LANES, MAP_SPEC, MAP_SPEC] + [W_SPEC, T_SPEC]
    return lon_call(longitude_third, specs, [SENT_PAIR], lon_scratch(128, 256), "longitude_third")(
        z, eta, first, ratio, *waves
    )[0]


def angle(product_of):
    return (product_of % NPHI).astype(F32) * (2.0 * math.pi / NPHI)


def wave_tables(slots, valid):
    scale = jnp.where(valid, NORMING, 0.0).astype(F32)
    tables = []
    for step, count in ((32, KP // 32), (1, 32)):
        phase = angle(jnp.arange(count, dtype=jnp.int32)[:, None] * step * slots[None, :])
        tables.append(jnp.stack([jnp.cos(phase), jnp.sin(phase)]) * (scale[None, None, :] if step > 1 else 1.0))
    for step in (128, 1):
        phase = angle(jnp.arange(128, dtype=jnp.int32)[None, :] * step * slots[:, None])
        tables.append(jnp.stack([jnp.cos(phase), jnp.sin(phase)]) * (scale[None, :, None] if step > 1 else 1.0))
    return tables


def fill_waves(coarse_ref, fine_ref, tcoarse_ref, tfine_ref, w_ref, t_ref):
    i = pl.program_id(0)
    cb, sb = fine_ref[0], fine_ref[1]
    for j in range(4):
        ca, sa = [coarse_ref[part, pl.ds(4 * i + j, 1), :] for part in range(2)]
        k = lax.broadcasted_iota(jnp.int32, (32, SA), 0) + (128 * i + 32 * j)
        keep = k <= NPHI // 2
        rows = pl.ds(32 * j, 32)
        for value, high, low in ((ca * cb - sa * sb, 0, 1), (sa * cb + ca * sb, 2, 3)):
            value = jnp.where(keep, value, 0.0)
            head = value.astype(BF16)
            w_ref[high, rows, :] = head
            w_ref[low, rows, :] = (value - head.astype(F32)).astype(BF16)
    cb, sb = tfine_ref[0], tfine_ref[1]
    for j in range(KP // 128):
        ca, sa = tcoarse_ref[0][:, j : j + 1], tcoarse_ref[1][:, j : j + 1]
        k = lax.broadcasted_iota(jnp.int32, (1, 128), 1) + 128 * j
        fold = jnp.where((k == 0) | (k == NPHI // 2), 0.5, jnp.where(k < NPHI // 2, 1.0, 0.0))
        cols = pl.ds(128 * j, 128)
        for value, high, low in ((ca * cb - sa * sb, 0, 1), (sa * cb + ca * sb, 2, 3)):
            value = value * fold
            head = value.astype(BF16)
            t_ref[high, :, cols] = head
            t_ref[low, :, cols] = (value - head.astype(F32)).astype(BF16)


def make_waves(tables):
    slot_rows = pl.BlockSpec((2, 128, 128), lambda i: (0, i, 0))
    return pl.pallas_call(
        fill_waves,
        grid=(KP // 128,),
        in_specs=[whole(2, KP // 32, SA), whole(2, 32, SA), slot_rows, slot_rows],
        out_specs=[pl.BlockSpec((4, 128, SA), lambda i: (0, i, 0))] * 2,
        out_shape=[pltpu.HBM((4, KP, SA), BF16)] * 2,
        compiler_params=params(),
        cost_estimate=cost(32 * KP * SA, 16 * KP * SA),
        name="fill_waves",
    )(*tables)


def fold_weights():
    k = jnp.arange(KP)
    half = NPHI // 2
    return jnp.where((k == 0) | (k == half), 0.5, jnp.where(k < half, 1.0, 0.0)).astype(F32)


def pad_cycles(x):
    lead = x.shape[:-1]
    x = x.reshape(lead + (2, 48))
    return jnp.pad(x, [(0, 0)] * len(lead) + [(0, 0), (0, 16)]).reshape(lead + (128,))


def pad_degrees(x):
    return jnp.pad(x, [(0, 0)] * (x.ndim - 1) + [(0, LP - L)])


def ord_exchange(x):
    return lax.all_to_all(x, "ord", split_axis=0, concat_axis=0, tiled=True)


def ord_gather(x):
    return ord_exchange(jnp.broadcast_to(x[None], (ORD,) + x.shape))


def core_swap(x):
    return lax.ppermute(x, "lat", [(i, i ^ 1) for i in range(LAT)])


def z_shift(x, step):
    return lax.ppermute(x, "lat", [(i, (i + 2 * step) % LAT) for i in range(LAT)])


def core_sum(parts, core):
    mine = lax.dynamic_index_in_dim(parts, core, 0, keepdims=False)
    away = lax.dynamic_index_in_dim(parts, 1 - core, 0, keepdims=False)
    return mine + core_swap(away)


def turn_blocks(x, count):
    return jnp.concatenate([x[count * ZB :], x[: count * ZB]], axis=0)


def lat_sum_small(parts, core):
    mine = core_sum(parts, core)
    there = [z_shift(mine, step) for step in range(1, 4)]
    total = mine
    for step in range(1, 4):
        total = total + turn_blocks(there[step - 1], step)
    return total, core_swap(total)


def lat_sum_large(high, low, core):
    high = core_sum(high, core)
    there = z_shift(high[:ZB], 2), z_shift(high[ZB:], 3)
    low = core_sum(low, core)
    own = low[:ZB] + there[0] + z_shift(low[ZB:], 1) + there[1]
    blocks = [own, z_shift(own, 3), z_shift(own, 2), z_shift(own, 1)]
    others = [core_swap(x) for x in blocks]
    return [(jnp.concatenate(blocks, axis=0), jnp.concatenate(others, axis=0))]


def after(x, *done):
    return lax.optimization_barrier((x,) + done)[0]


def shards(grid_field, legendre, cycle_weight, slot_order, kappa, eta, pairs, target):
    me = lax.axis_index("ord")
    z, core = lax.axis_index("lat") // 2, lax.axis_index("lat") % 2
    info = jnp.stack([z, core]).astype(jnp.int32)
    direction = me % 4

    field = jnp.pad(pad_cycles(grid_field), [(0, 6), (0, 0)])
    field_all = ord_gather(field).reshape(ORD * 96, 128)

    position = jnp.arange(SP, dtype=jnp.int32)
    quad = quad_index(position // SB, position // 4 % 2, z)
    place = quad * 4 + position % 4
    slots2 = jnp.pad(slot_order.reshape(ORD, SLOT), [(0, 0), (0, SP - SLOT)])
    slots2 = jnp.sum(jnp.where(place[None, :, None] == position[None, None, :], slots2[:, None, :], 0), axis=2)
    own_valid = place < SLOT
    slots = slots2.reshape(SA)
    valid = jnp.broadcast_to(own_valid, (ORD, SP)).reshape(SA)
    my_slots = lax.dynamic_index_in_dim(slots2, me, 0, keepdims=False)
    degree_ids = jnp.arange(L, dtype=jnp.int32)
    info = jnp.concatenate([info, jnp.where(own_valid, my_slots, L)])
    table = jnp.transpose(legendre, (1, 0, 2))

    offset = jnp.arange(96, dtype=jnp.int32)
    longitude = (jnp.arange(ORD, dtype=jnp.int32)[:, None] * 90 + offset[None, :]).reshape(ORD * 96)
    k_valid = jnp.broadcast_to(offset < 90, (ORD, 96)).reshape(ORD * 96)
    phase = angle(my_slots[:, None] * longitude[None, :])
    own_scale = jnp.where(own_valid[:, None] & k_valid[None, :], NORMING, 0.0).astype(F32)
    own_waves = jnp.stack([jnp.cos(phase) * own_scale, jnp.sin(phase) * own_scale]).reshape(2 * SP, ORD * 96)

    weight_lanes = pad_cycles(cycle_weight[None, :])
    spectra = jnp.dot(own_waves, field_all, precision=HIGHEST_PREC).reshape(2, SP, 128)
    parts = run_analysis_one(info, spectra, weight_lanes, table)

    eta_rows = lax.dynamic_index_in_dim(eta, direction, 0, keepdims=False)
    hit = slots[:, None] == degree_ids[None, :]
    eta_cols = [jnp.sum(jnp.where(hit, eta_rows[r][None, :], 0.0), axis=1, keepdims=True) for r in range(2)]
    eta_lanes = jnp.where(jnp.arange(128)[None, :] < 64, eta_cols[0], eta_cols[1])

    scale_ids = jnp.arange(kappa.shape[0], dtype=jnp.int32)
    picks = [(pairs[:, i : i + 1] == scale_ids[None, :]).astype(F32) for i in range(2)]
    kaps = [pad_degrees(jnp.sum(pick[:, :, None] * kappa[None], axis=1)) for pick in picks]
    kap_rows = jnp.stack([jnp.repeat(kap, 4, axis=0) for kap in kaps])
    kap_second = kap_rows[1]
    target_rows = target.reshape(8, 1)
    ones = jnp.ones((1, 128), F32)
    my_weight = lax.dynamic_index_in_dim(weight_lanes.reshape(2, 64), me // 8, 0, keepdims=True)
    my_weight = jnp.concatenate([my_weight, my_weight], axis=1)
    fold_lanes = jnp.broadcast_to(fold_weights()[:, None], (KP, 128))

    def all_sums(x, w, carry):
        high = run_analysis_fields(info, x, w, table, HALF, HALF, carry)
        low = run_analysis_fields(info, x, after(w, high), table, 0, HALF, carry)
        return lat_sum_large(high, low, core)

    mine, other = lat_sum_small(parts, core)
    cycles = run_synthesis_base(info, mine, other, kap_rows, table)
    z_first = ord_exchange(cycles)
    waves = make_waves(after(wave_tables(slots, valid), cycles))
    spectra, first_maps, pair_maps = run_longitude_first(z_first, eta_lanes, waves)
    sums = all_sums(ord_exchange(spectra), weight_lanes, False)
    z_second = ord_exchange(run_synthesis_fields(info, sums, kap_second, ones, table, target_rows, False))
    spectra, ratio = run_longitude_second(z_second, eta_lanes, my_weight, fold_lanes, pair_maps, waves)
    sums = all_sums(ord_exchange(spectra), ones, True)
    z_third = ord_exchange(run_synthesis_fields(info, sums, kap_second, weight_lanes, table, target_rows, True))
    spectra = run_longitude_third(z_third, eta_lanes, first_maps, ratio, waves)
    mine, other = lat_sum_small(run_analysis_sum(info, ord_exchange(spectra), kap_rows, table), core)
    cycles = run_synthesis_last(info, mine, other, weight_lanes, table)

    end_slots = after(slots, z_third)
    phase = angle((me * 90 + offset)[:, None] * end_slots[None, :])
    end_scale = jnp.where(valid[None, :], NORMING, 0.0).astype(F32)
    end_waves = jnp.stack(
        [(jnp.cos(phase) * end_scale).reshape(96, ORD, SP), (jnp.sin(phase) * end_scale).reshape(96, ORD, SP)], axis=2
    ).reshape(96, ORD * 2 * SP)
    cycles_all = ord_gather(cycles.reshape(2 * SP, 128)).reshape(ORD * 2 * SP, 128)
    result = jnp.dot(end_waves, cycles_all, precision=HIGHEST_PREC)
    return result[:90].reshape(90, 2, 64)[:, :, :48].reshape(90, 96)


def solution(mesh):
    return jax.shard_map(
        shards,
        mesh=mesh,
        in_specs=(P("ord", "lat"), P("lat", "ord", None), P("lat"), P(), P(), P(), P(), P()),
        out_specs=P("ord", "lat"),
        check_vma=False,
    )
```
